128 devices in a mesh: node: 8 (over y, core), cores: 16 (over z, x).
Axes of the slice: x: 4, y: 4, z: 4, core: 2. Of those that a mesh axis runs over, the one named last changes fastest.
Arguments:
- adjoint: bfloat16 [1024, 2, 128, 128], P(('node', 'cores')), may hold values from -6 to 6
- saved: bfloat16 [2, 4, 1024, 2, 128, 128], P(None, None, ('node', 'cores')), may hold values from -0.046875 to 0.046875
- propagators: bfloat16 [2, 4, 2, 128, 128], replicated, may hold values from -3 to 3, as said below
- coupling: bfloat16 [128, 128], replicated, may hold values from -0.5 to 0.5
- higher: int32 [1024, 4], replicated, may hold values from 0 to 1023, as said below
- lower: int32 [1024, 4], replicated, may hold values from 0 to 1023, as said below
- ladder: int32 [2, 1024, 4], P(None, ('node', 'cores')), may hold values from 0 to 3
- rates: float32 [2, 4], replicated, may hold values from 0.1 to 0.4
- decay: float32 [1024], P(('node', 'cores')), may hold values from 0.4 to 1
Outputs:
- adjoint_out: bfloat16 [1024, 2, 128, 128], P(('node', 'cores'))
- gradient: float32 [128, 8, 2, 128], P(('node', 'cores'))
The draws below stay inside these ranges and needn't reach their ends.
Inputs may be any that keep to these rules, and one draw needn't show every extreme that they name: Density j lives on owner j // 8. Taken in the order of density then mode, the 32 higher-tier partners of one owner's densities lie on distinct owners when 8 * 4 <= 128, and else exactly 1 of them lie on each owner. The same holds for the lower-tier partners. `propagators`: A propagator substep is close to unitary.
All inputs are finite; a program needn't handle non-finite values.
Results may differ from the reference program's by a relative error of at most 0.024.
Values may be sent and summed in bfloat16 or wider, within the bound.
No kernel may reach another device: no remote copies, remote signals or barrier semaphores. Data moves between devices by JAX's collectives and lax.ppermute only.
A program may use at most 128 MiB of HBM per device.

```python
import math
import jax
import jax.numpy as jnp

DIM = 128
MODES = 4
ADO_DEV = 8
STEPS = 2
NSUB = 4
OWNERS = 128
NA = 1024


def build_partners(key):
    links = ADO_DEV * MODES
    perm_key = jax.random.fold_in(key, 11)
    local_key = jax.random.fold_in(key, 12)
    perms = jax.vmap(lambda owner_id: jax.random.permutation(jax.random.fold_in(perm_key, owner_id), OWNERS))(jnp.arange(OWNERS))
    source = perms[:, jnp.arange(links) % OWNERS]
    local = jax.random.randint(local_key, (OWNERS, links), 0, ADO_DEV)
    return (source * ADO_DEV + local).reshape(OWNERS * ADO_DEV, MODES).astype(jnp.int32)


def draw_higher(key, part):
    return build_partners(jax.random.fold_in(key, 1))


def draw_lower(key, part):
    return build_partners(jax.random.fold_in(key, 2))


def draw_propagators(key, part):
    scale = 0.4 / DIM ** 0.5
    raw = jax.random.normal(key, (STEPS, NSUB, DIM, DIM), jnp.float32) * scale
    hermit = (raw + jnp.swapaxes(raw, -1, -2)) / 2.0 ** 0.5
    square = jnp.matmul(hermit, hermit)
    cube = jnp.matmul(square, hermit)
    identity = jnp.eye(DIM, dtype=jnp.float32)
    real_part = identity - 0.5 * square
    imag_part = -hermit + cube / 6.0
    return jnp.stack([real_part, imag_part], axis=2).astype(jnp.bfloat16)


def set_ends(values, own_key, least, high):
    extent = values.shape
    index_at = [jax.random.randint(jax.random.fold_in(own_key, axis), (), 0, extent[axis]) for axis in range(len(extent))]
    values = values.at[tuple(index_at)].set(least)
    longest = extent.index(max(extent))
    index_at[longest] = (index_at[longest] + 1) % extent[longest]
    return values.at[tuple(index_at)].set(high)


def with_spikes(array, rng, source, target, parts, factor):
    def block_of(position):
        return (jnp.arange(array.shape[position]) // (array.shape[position] // parts)).reshape((-1,) + (1,) * (array.ndim - 1 - position))

    first = jax.random.permutation(rng, parts)[block_of(target)]
    other_side = (block_of(target) + parts // 2) % parts
    return jnp.where((block_of(source) == first) | (block_of(source) == other_side), factor * array, array)


def level_of(key, extent, pieces, smallest, high):
    gain = 1.0
    for position, blocks in pieces:
        draws = jax.random.uniform(jax.random.fold_in(jax.random.fold_in(key, 6), position), (blocks,), jnp.float32, smallest / len(pieces), high / len(pieces))
        gain = gain * jnp.repeat(jnp.exp(draws), extent[position] // blocks).reshape((-1,) + (1,) * (len(extent) - 1 - position))
    return gain


def centred(rng, shape, deviation, bound, pieces=(), kind=jnp.bfloat16):
    gain = level_of(rng, shape, pieces, -0.22, 0.18) if pieces else 1.0
    drawn = jax.random.normal(rng, shape, jnp.float32) * deviation * gain
    return jnp.minimum(jnp.maximum(drawn, -bound), bound).astype(kind)


def gaussian_with(own_key, shape, width, limit, pieces, heavy, kind=jnp.bfloat16):
    entries = width * jax.random.normal(own_key, shape, jnp.float32)
    if pieces:
        entries = entries * level_of(own_key, shape, pieces, -0.22, 0.18)
    return jnp.clip(with_spikes(entries, jax.random.fold_in(own_key, 3), *heavy), -limit, limit).astype(kind)


def setup_inputs(seed: int = 0) -> dict:
    key_list = jax.random.split(jax.random.key(seed), 10)
    return {
        "adjoint": centred(key_list[0], (NA, 2, DIM, DIM), 1.0, 6.0, ((0, 128),)),
        "saved": gaussian_with(key_list[1], (STEPS, NSUB, NA, 2, DIM, DIM), (1.0 / (2 * DIM * NA) ** 0.5), 0.046875, ((2, 128),), (2, 5, 128, 5.5)),
        "propagators": draw_propagators(jax.random.fold_in(key_list[9], 71), 0),
        "coupling": centred(key_list[3], (DIM, DIM), DIM ** -0.5, 0.5),
        "higher": draw_higher(jax.random.fold_in(key_list[9], 71), 0),
        "lower": draw_lower(jax.random.fold_in(key_list[9], 71), 0),
        "ladder": set_ends(jax.random.randint(key_list[6], (2, NA, MODES), 0, 4), jax.random.fold_in(key_list[6], 1), 0, 3).astype(jnp.int32),
        "rates": jnp.clip(jnp.exp(jax.random.uniform(key_list[7], (2, MODES), jnp.float32, math.log(0.1), math.log(0.4))), 0.1, 0.4),
        "decay": jnp.clip(0.4 + 0.6 * jax.random.uniform(key_list[8], (NA,), jnp.float32) ** level_of(key_list[8], (NA,), ((0, 128),), -0.2, 0.2), 0.4, 1.0),
    }


def linked_sum(state_full, link_table, weights, strengths):
    total = jnp.zeros(state_full.shape, jnp.float32)
    for mode_index in range(MODES):
        factor = weights[:, mode_index].astype(jnp.float32) * strengths[mode_index]
        total = total + factor[:, None, None, None] * state_full[link_table[:, mode_index]]
    return total


def couple_step(state, up_sum, down_sum, coupling, decay):
    plus = (up_sum + down_sum).astype(jnp.bfloat16).astype(jnp.float32)
    minus = (up_sum - down_sum).astype(jnp.bfloat16).astype(jnp.float32)
    operator = coupling.astype(jnp.float32)
    left = jnp.einsum('ab,jxbc->jxac', operator, plus)
    right = jnp.einsum('jxab,bc->jxac', minus, operator)
    kept = decay[:, None, None, None] * state.astype(jnp.float32)
    real_part = kept[:, 0] + left[:, 1] - right[:, 1]
    imag_part = kept[:, 1] - left[:, 0] + right[:, 0]
    return jnp.stack([real_part, imag_part], axis=1).astype(jnp.bfloat16)


def rotate_step(state, prop_re, prop_im):
    state_f = state.astype(jnp.float32)
    real_u = prop_re.astype(jnp.float32)
    imag_u = prop_im.astype(jnp.float32)
    times_re = jnp.einsum('jxab,bc->jxac', state_f, real_u)
    times_im = jnp.einsum('jxab,bc->jxac', state_f, imag_u)
    middle = jnp.stack([times_re[:, 0] - times_im[:, 1], times_im[:, 0] + times_re[:, 1]], axis=1)
    middle = middle.astype(jnp.bfloat16).astype(jnp.float32)
    left_re = jnp.einsum('ba,jxbc->jxac', real_u, middle)
    left_im = jnp.einsum('ba,jxbc->jxac', imag_u, middle)
    result = jnp.stack([left_re[:, 0] + left_im[:, 1], left_re[:, 1] - left_im[:, 0]], axis=1)
    return result.astype(jnp.bfloat16)


def projection(saved_block, state):
    saved_f = saved_block.astype(jnp.float32)
    state_f = state.astype(jnp.float32)
    swapped = jnp.stack([state_f[:, 1], -state_f[:, 0]], axis=1)
    real_part = jnp.einsum('jxba,jxbc->ac', saved_f, state_f)
    imag_part = jnp.einsum('jxba,jxbc->ac', saved_f, swapped)
    return jnp.stack([real_part, imag_part], axis=1)


def reference(adjoint, saved, propagators, coupling, higher, lower, ladder, rates, decay):
    state = adjoint
    columns = []
    for step_index in range(STEPS):
        state_full = state.astype(jnp.float32)
        up_sum = linked_sum(state_full, higher, ladder[0], rates[0])
        down_sum = linked_sum(state_full, lower, ladder[1], rates[1])
        state = couple_step(state, up_sum, down_sum, coupling, decay)
        for substep in range(NSUB):
            state = rotate_step(state, propagators[step_index, substep, 0], propagators[step_index, substep, 1])
            columns.append(projection(saved[step_index, substep], state))
    return state, jnp.stack(columns, axis=1)
```

```python
import jax
import jax.numpy as jnp
from jax import lax
from jax.experimental import pallas as pl
from jax.experimental.pallas import tpu as pltpu
from jax.sharding import Mesh
from jax.sharding import PartitionSpec as P

AXES = ("y", "c", "z", "x")
BF = jnp.bfloat16
F32 = jnp.float32
OWN = 8
MODES = 4
DIM = 128
ROWS = 2 * DIM
BLOCK = OWN * ROWS


def pairs(move):
    out = []
    for y in range(4):
        for c in range(2):
            for z in range(4):
                for x in range(4):
                    ny, nc, nz, nx = move(y, c, z, x)
                    here = ((y * 2 + c) * 4 + z) * 4 + x
                    there = ((ny * 2 + nc) * 4 + nz) * 4 + nx
                    out.append((here, there))
    return out


def first(s):
    return pairs(lambda y, c, z, x: (y, c, z, (x + s) % 4) if c == 0 else (y, c, (z + s) % 4, x))


def second(s):
    return pairs(lambda y, c, z, x: (y, c, (z + s) % 4, x) if c == 0 else (y, c, z, (x + s) % 4))


def along_y(s):
    return pairs(lambda y, c, z, x: ((y + s) % 4, c, z, x))


def along_z(s):
    return pairs(lambda y, c, z, x: (y, c, (z + s) % 4, x))


def along_x(s):
    return pairs(lambda y, c, z, x: (y, c, z, (x + s) % 4))


SIBLING = pairs(lambda y, c, z, x: (y, 1 - c, z, x))


def send(a, route):
    return lax.ppermute(a, AXES, route)


def gather_layer(block):
    near = {0: block}
    for s in (1, 3, 2):
        near[s] = send(block, first(s))
    held = {}
    for s in (0, 1, 3, 2):
        held[s, 0] = near[s]
        held[s, 1] = send(near[s], second(1))
        held[s, 3] = send(near[s], second(3))
        if s in (0, 3):
            held[s, 2] = send(held[s, 1], second(1))
        else:
            held[s, 2] = send(held[s, 3], second(3))
    mine = [held[s, t] for s in range(4) for t in range(4)]
    return mine + [send(b, SIBLING) for b in mine]


def gather_meta(meta):
    by_y = jnp.stack([meta] + [send(meta, along_y(s)) for s in (1, 2, 3)])
    part = by_y.reshape(32, 16)
    part = jnp.concatenate([part, send(part, SIBLING)])
    part = jnp.concatenate([part] + [send(part, along_z(s)) for s in (1, 2, 3)])
    part = jnp.concatenate([part] + [send(part, along_x(s)) for s in (1, 2, 3)])
    return by_y, part


def slot_of(q, at):
    y, c, z, x = at
    owner = q >> 3
    oy, oc, oz, ox = owner >> 5, (owner >> 4) & 1, (owner >> 2) & 3, owner & 3
    dx, dz = (x - ox) & 3, (z - oz) & 3
    s = jnp.where(oc == 0, dx, dz)
    t = jnp.where(oc == 0, dz, dx)
    other = (oc != c).astype(jnp.int32)
    slot = ((other * 16 + s * 4 + t) << 3) + (q & 7)
    return jnp.where(oy == y, slot, -1)


def meta_row(q, at):
    y, c, z, x = at
    owner = q >> 3
    oy, oc, oz, ox = owner >> 5, (owner >> 4) & 1, (owner >> 2) & 3, owner & 3
    other = (oc != c).astype(jnp.int32)
    relative = ((((x - ox) & 3) * 4 + ((z - oz) & 3)) * 2 + other) * 4 + ((y - oy) & 3)
    return (relative << 3) + (q & 7)


def compact(slot, values):
    count = slot.shape[-1]
    keep = (slot >= 0) & (values[0] != 0)
    before = jnp.arange(count)[:, None] < jnp.arange(count)[None, :]
    at = jnp.sum((keep[..., :, None] & before).astype(jnp.int32), axis=-2)
    moved = keep[..., :, None] & (at[..., :, None] == jnp.arange(count))
    lists = [jnp.sum(jnp.where(moved, v[..., :, None], 0), axis=-2).reshape(-1) for v in [slot, *values]]
    return [jnp.sum(keep.astype(jnp.int32), axis=-1).reshape(-1), *lists]


def pick(rows, table):
    hot = (rows.reshape(-1)[:, None] == jnp.arange(table.shape[0])[None, :]).astype(F32)
    return jnp.dot(hot, table, precision=lax.Precision.HIGHEST, preferred_element_type=F32)


def own_links(higher, lower, at):
    y, c, z, x = at
    rows = []
    for dy in range(4):
        start = ((((y + dy) & 3) * 2 + c) * 16 + z * 4 + x) * OWN
        both = [lax.dynamic_slice_in_dim(t, start, OWN, 0) for t in (higher, lower)]
        rows.append(jnp.concatenate(both, axis=1))
    return jnp.concatenate(rows)


def link_lists(higher, lower, by_y, meta, rates, at):
    strengths = rates.reshape(1, 8)
    partner = own_links(higher, lower, at)
    weights = jnp.concatenate([by_y[0], by_y[3], by_y[2], by_y[1]])[:, :8] * strengths
    near_slot = slot_of(partner, at)
    wanted = pick(meta_row(partner, at), meta)
    decay = wanted[:, 8].reshape(32, 8)
    near = compact(near_slot.reshape(32, 2, 4), [v.reshape(32, 2, 4) for v in (weights, weights * decay)])
    far = jnp.concatenate([slot_of(higher, at), slot_of(lower, at)], axis=1).astype(F32)
    far_slot = pick(partner, far).astype(jnp.int32)
    far_weight = wanted[:, :8] * strengths * weights.reshape(256, 1)
    spread = lambda v: v.reshape(32, 2, 4, 2, 4).transpose(0, 1, 3, 2, 4).reshape(32, 4, 16)
    return near, compact(spread(far_slot), [spread(far_weight)])


def fetch(blocks, held, sems):
    copies = [
        pltpu.make_async_copy(b, held.at[pl.ds(k * BLOCK, BLOCK), :], sems.at[k])
        for k, b in enumerate(blocks)
    ]
    for copy in copies:
        copy.start()
    for copy in copies:
        copy.wait()


def link_sum(held, slots, weights, base, count):
    def add(k, total):
        start = pl.multiple_of(slots[base + k] * ROWS, ROWS)
        return total + weights[base + k] * held[pl.ds(start, ROWS), :].astype(F32)

    return lax.fori_loop(0, count, add, jnp.zeros((ROWS, DIM), F32))


def mm(a, b):
    return jnp.dot(a, b, preferred_element_type=F32)


def commute(c, plus, minus):
    left = mm(c, jnp.concatenate([plus[DIM:], -plus[:DIM]], axis=1))
    right = mm(minus, c)
    return left[:, :DIM] - right[DIM:], left[:, DIM:] + right[:DIM]


def near_kernel(count, slots, weights, c_ref, *refs):
    blocks, outs = refs[:32], refs[32:36]
    held, sems = refs[36:]
    fetch(blocks, held, sems)
    c = c_ref[...]
    for dy in range(4):
        out = outs[dy]

        def one(i, _):
            d = (dy * OWN + i) * 2
            up = link_sum(held, slots, weights, d * 4, count[d])
            down = link_sum(held, slots, weights, d * 4 + 4, count[d + 1])
            re, im = commute(c, (up + down).astype(BF), (up - down).astype(BF))
            at = pl.multiple_of(i * ROWS, ROWS)
            out[pl.ds(at, DIM), :] = re.astype(out.dtype)
            out[pl.ds(at + DIM, DIM), :] = im.astype(out.dtype)
            return 0

        lax.fori_loop(0, OWN, one, 0)


def far_kernel(n1, s1, w1, n2, s2, w2, c_ref, right_ref, left_ref, *refs):
    blocks, outs = refs[:32], refs[32:36]
    held, sems, acc = refs[36:]
    fetch(blocks, held, sems)
    c = c_ref[...]
    for dy in range(4):
        out = outs[dy]

        def one(i, _):
            d = dy * OWN + i
            for k in range(4):
                acc[k] = link_sum(held, s2, w2, d * 64 + k * 16, n2[d * 4 + k])
            for k in range(2):
                acc[4 + k] = link_sum(held, s1, w1, d * 8 + k * 4, n1[d * 2 + k])
            pu, mu = acc[0] + acc[1], acc[0] - acc[1]
            pd, md = acc[2] + acc[3], acc[2] - acc[3]
            halves = []
            for sign in (1, -1):
                re, im = commute(c, (pu + sign * pd).astype(BF), (mu + sign * md).astype(BF))
                kept = acc[4] + sign * acc[5]
                halves.append(jnp.concatenate([kept[:DIM] + re, kept[DIM:] + im], axis=1))
            y = jnp.concatenate(halves).astype(BF)
            mid = mm(y, right_ref[...]).astype(BF)
            stacked = jnp.concatenate(
                [
                    jnp.concatenate([mid[:DIM, :DIM], mid[DIM:, :DIM]], axis=1),
                    jnp.concatenate([mid[:DIM, DIM:], mid[DIM:, DIM:]], axis=1),
                ]
            )
            turned = mm(left_ref[...], stacked).astype(BF)
            re, im = commute(c, turned[:, :DIM], turned[:, DIM:])
            at = pl.multiple_of(i * ROWS, ROWS)
            out[pl.ds(at, DIM), :] = re.astype(out.dtype)
            out[pl.ds(at + DIM, DIM), :] = im.astype(out.dtype)
            return 0

        lax.fori_loop(0, OWN, one, 0)


SM = pl.BlockSpec(memory_space=pltpu.SMEM)
VM = pl.BlockSpec(memory_space=pltpu.VMEM)
ANY = pl.BlockSpec(memory_space=pl.ANY)


def parts_of(kernel, scalars, arrays, blocks, scratch, flops):
    shapes = [jax.ShapeDtypeStruct((BLOCK, DIM), F32)] + [jax.ShapeDtypeStruct((BLOCK, DIM), BF)] * 3
    return pl.pallas_call(
        kernel,
        out_shape=shapes,
        in_specs=[SM] * len(scalars) + [VM] * len(arrays) + [ANY] * 32,
        out_specs=[VM] * 4,
        scratch_shapes=[pltpu.VMEM((32 * BLOCK, DIM), BF), pltpu.SemaphoreType.DMA((32,))] + scratch,
        compiler_params=pltpu.CompilerParams(vmem_limit_bytes=32 << 20),
        cost_estimate=pl.CostEstimate(flops=flops, bytes_accessed=20 << 20, transcendentals=0),
    )(*scalars, *arrays, *blocks)


def chain_kernel(decay, lam_ref, own_ref, a_ref, b_ref, d_ref, right_ref, left_ref, saved_ref, out_ref, grad_ref, wide, tall):
    for j in range(OWN):
        rows = pl.ds(j * ROWS, ROWS)
        mixed = decay[j] * lam_ref[rows, :].astype(F32) + own_ref[rows, :]
        mixed = mixed + a_ref[rows, :].astype(F32) + b_ref[rows, :].astype(F32) + d_ref[rows, :].astype(F32)
        mixed = mixed.astype(BF)
        wide[pl.ds(j * DIM, DIM), 0:DIM] = mixed[:DIM]
        wide[pl.ds(j * DIM, DIM), DIM:ROWS] = mixed[DIM:]

    def substep(u, _):
        right, left = right_ref[u], left_ref[u]
        for h in range(OWN // 2):
            mid = mm(wide[pl.ds(h * ROWS, ROWS), :], right).astype(BF)
            stacked = jnp.concatenate(
                [
                    jnp.concatenate([mid[:DIM, :DIM], mid[DIM:, :DIM]], axis=1),
                    jnp.concatenate([mid[:DIM, DIM:], mid[DIM:, DIM:]], axis=1),
                ]
            )
            turned = mm(left, stacked).astype(BF)
            for k in range(2):
                re, im = turned[:DIM, k * DIM : (k + 1) * DIM], turned[DIM:, k * DIM : (k + 1) * DIM]
                j = 2 * h + k
                wide[pl.ds(j * DIM, DIM), 0:DIM] = re
                wide[pl.ds(j * DIM, DIM), DIM:ROWS] = im
                tall[pl.ds(j * ROWS, DIM), 0:DIM] = re
                tall[pl.ds(j * ROWS, DIM), DIM:ROWS] = im
                tall[pl.ds(j * ROWS + DIM, DIM), 0:DIM] = im
                tall[pl.ds(j * ROWS + DIM, DIM), DIM:ROWS] = -re
        terms = lax.dot_general(
            saved_ref[u], tall[...], (((0,), (0,)), ((), ())), preferred_element_type=F32
        )
        grad_ref[u, 0] = terms[:, :DIM]
        grad_ref[u, 1] = terms[:, DIM:]
        return 0

    lax.fori_loop(0, 4, substep, 0)
    for j in range(OWN):
        out_ref[pl.ds(j * ROWS, DIM), :] = wide[pl.ds(j * DIM, DIM), 0:DIM]
        out_ref[pl.ds(j * ROWS + DIM, DIM), :] = wide[pl.ds(j * DIM, DIM), DIM:ROWS]


def chain(decay, lam, parts, right, left, saved):
    return pl.pallas_call(
        chain_kernel,
        out_shape=[
            jax.ShapeDtypeStruct((BLOCK, DIM), BF),
            jax.ShapeDtypeStruct((4, 2, DIM, DIM), F32),
        ],
        in_specs=[SM] + [VM] * 8,
        out_specs=[VM] * 2,
        scratch_shapes=[pltpu.VMEM((OWN * DIM, ROWS), BF), pltpu.VMEM((BLOCK, ROWS), BF)],
        compiler_params=pltpu.CompilerParams(vmem_limit_bytes=24 << 20),
        cost_estimate=pl.CostEstimate(flops=2 * 10**9, bytes_accessed=6 << 20, transcendentals=0),
    )(decay, lam, *parts, right, left, saved)


def compose_kernel(prop_ref, right_ref, left_ref):
    hi = lambda v: v.astype(BF)
    re, im = prop_ref[0, 0].astype(F32), prop_ref[0, 1].astype(F32)
    for u in range(1, 4):
        ur, ui = prop_ref[u, 0], prop_ref[u, 1]
        mul = lambda v, m: mm(hi(v), m) + mm(hi(v - hi(v).astype(F32)), m)
        re, im = mul(re, ur) - mul(im, ui), mul(re, ui) + mul(im, ur)
    turned_re, turned_im = re.T.astype(BF), im.T.astype(BF)
    re, im = re.astype(BF), im.astype(BF)
    right_ref[0:DIM, 0:DIM] = re
    right_ref[0:DIM, DIM:ROWS] = im
    right_ref[DIM:ROWS, 0:DIM] = -im
    right_ref[DIM:ROWS, DIM:ROWS] = re
    left_ref[0:DIM, 0:DIM] = turned_re
    left_ref[0:DIM, DIM:ROWS] = turned_im
    left_ref[DIM:ROWS, 0:DIM] = -turned_im
    left_ref[DIM:ROWS, DIM:ROWS] = turned_re


def compose(props):
    return pl.pallas_call(
        compose_kernel,
        out_shape=[jax.ShapeDtypeStruct((ROWS, ROWS), BF)] * 2,
        in_specs=[VM],
        out_specs=[VM] * 2,
    )(props)


def body(adjoint, saved, propagators, coupling, higher, lower, ladder, rates, decay):
    at = tuple(lax.axis_index(a) for a in AXES)
    lam = adjoint.reshape(BLOCK, DIM)
    meta = jnp.concatenate(
        [ladder[0].astype(F32), ladder[1].astype(F32), decay[:, None], jnp.zeros((OWN, 7), F32)], axis=1
    )
    blocks = gather_layer(lam)
    by_y, meta = gather_meta(meta)
    near, far = link_lists(higher, lower, by_y, meta, rates, at)
    count, slots, weights, damped = near
    re, im = propagators[:, :, 0], propagators[:, :, 1]
    right = jnp.concatenate(
        [jnp.concatenate([re, im], axis=3), jnp.concatenate([-im, re], axis=3)], axis=2
    )
    turn = lambda v: jnp.swapaxes(v, 2, 3)
    left = jnp.concatenate(
        [jnp.concatenate([turn(re), turn(im)], axis=3), jnp.concatenate([-turn(im), turn(re)], axis=3)], axis=2
    )
    whole_right, whole_left = compose(propagators[0])
    one = parts_of(near_kernel, [count, slots, weights], [coupling], blocks, [], 10**9)
    got_one = [one[0]] + [send(one[dy], along_y(dy)) for dy in (1, 2, 3)]
    two = parts_of(
        far_kernel,
        [count, slots, damped, *far],
        [coupling, whole_right, whole_left],
        blocks,
        [pltpu.VMEM((6, ROWS, DIM), F32)],
        16 * 10**9,
    )
    got_two = [two[0]] + [send(two[dy], along_y(dy)) for dy in (1, 2, 3)]
    saved = saved.reshape(2, 4, BLOCK, DIM)
    lam, grad_one = chain(decay, lam, got_one, right[0], left[0], saved[0])
    lam, grad_two = chain(decay, lam, got_two, right[1], left[1], saved[1])
    grad = jnp.concatenate([grad_one, grad_two]).astype(BF)
    grad = jnp.moveaxis(grad, 2, 0)
    grad = lax.all_to_all(grad, AXES, 0, 0, tiled=True)
    grad = jnp.sum(grad.astype(F32), axis=0, keepdims=True)
    return lam.reshape(OWN, 2, DIM, DIM), grad


def solution(mesh):
    finer = Mesh(mesh.devices.reshape(4, 2, 4, 4), AXES)
    rows = P(AXES)
    return jax.shard_map(
        body,
        mesh=finer,
        in_specs=(rows, P(None, None, AXES), P(), P(), P(), P(), P(None, AXES), P(), rows),
        out_specs=(rows, rows),
        check_vma=False,
    )
```

```python
import functools

import jax
import jax.numpy as jnp
from jax import lax
from jax.experimental import pallas as pl
from jax.experimental.pallas import tpu as pltpu
from jax.sharding import Mesh
from jax.sharding import PartitionSpec as P

AXES = ("y", "c", "z", "x")
BF = jnp.bfloat16
F32 = jnp.float32
OWN = 8
MODES = 4
DIM = 128
ROWS = 2 * DIM
BLOCK = OWN * ROWS
GROUP = 4
EXTRA = 64


def pairs(move):
    out = []
    for y in range(4):
        for c in range(2):
            for z in range(4):
                for x in range(4):
                    ny, nc, nz, nx = move(y, c, z, x)
                    here = ((y * 2 + c) * 4 + z) * 4 + x
                    there = ((ny * 2 + nc) * 4 + nz) * 4 + nx
                    out.append((here, there))
    return out


def first(s):
    return pairs(lambda y, c, z, x: (y, c, z, (x + s) % 4) if c == 0 else (y, c, (z + s) % 4, x))


def second(s):
    return pairs(lambda y, c, z, x: (y, c, (z + s) % 4, x) if c == 0 else (y, c, z, (x + s) % 4))


def along_y(s):
    return pairs(lambda y, c, z, x: ((y + s) % 4, c, z, x))


SIBLING = pairs(lambda y, c, z, x: (y, 1 - c, z, x))


def send(a, route):
    return lax.ppermute(a, AXES, route)


def gather_layer(block, prepare):
    near = {0: block}
    for s in (1, 3, 2):
        near[s] = send(block, first(s))
    made = prepare(near[3])
    near[2], made = lax.optimization_barrier((near[2], made))
    held = {}
    for s in (0, 1, 3, 2):
        held[s, 0] = near[s]
        held[s, 1] = send(near[s], second(1))
        held[s, 3] = send(near[s], second(3))
        if s in (0, 3):
            held[s, 2] = send(held[s, 1], second(1))
        else:
            held[s, 2] = send(held[s, 3], second(3))
    mine = [held[s, t] for s in range(4) for t in range(4)]
    return made, mine + [send(b, SIBLING) for b in mine]


def own_meta(ladder, decay):
    top = lax.reduce_precision(decay, 8, 7)
    mid = lax.reduce_precision(decay - top, 8, 7)
    parts = [ladder[0].astype(F32), ladder[1].astype(F32), jnp.stack([top, mid, decay - top - mid], axis=1)]
    return jnp.concatenate(parts, axis=1)


def place(q, at):
    y, c, z, x = at
    owner = q >> 3
    oy, oc, oz, ox = owner >> 5, (owner >> 4) & 1, (owner >> 2) & 3, owner & 3
    dx, dz = (x - ox) & 3, (z - oz) & 3
    s = jnp.where(oc == 0, dx, dz)
    t = jnp.where(oc == 0, dz, dx)
    other = (oc != c).astype(jnp.int32)
    return (y - oy) & 3, ((other * 16 + s * 4 + t) << 3) + (q & 7)


def slot_of(q, at):
    dy, slot = place(q, at)
    return jnp.where(dy == 0, slot, -1)


def compact(slot, values):
    count = slot.shape[-1]
    keep = (slot >= 0) & (values[0] != 0)
    before = jnp.arange(count)[:, None] < jnp.arange(count)[None, :]
    at = jnp.sum((keep[..., :, None] & before).astype(jnp.int32), axis=-2)
    moved = keep[..., :, None] & (at[..., :, None] == jnp.arange(count))
    lists = [jnp.sum(jnp.where(moved, v[..., :, None], 0), axis=-2).reshape(-1) for v in [slot, *values]]
    return [jnp.sum(keep.astype(jnp.int32), axis=-1).reshape(-1), *lists]


def pick(rows, table):
    hot = (rows.reshape(-1)[:, None] == jnp.arange(table.shape[0])[None, :]).astype(BF)
    return jnp.dot(hot, table.astype(BF), preferred_element_type=F32)


def own_links(higher, lower, at):
    y, c, z, x = at
    rows = []
    for dy in range(4):
        start = ((((y + dy) & 3) * 2 + c) * 16 + z * 4 + x) * OWN
        both = [lax.dynamic_slice_in_dim(t, start, OWN, 0) for t in (higher, lower)]
        rows.append(jnp.concatenate(both, axis=1))
    return jnp.concatenate(rows)


def near_lists(partner, weights, at):
    return compact(slot_of(partner, at).reshape(32, 2, 4), [weights.reshape(32, 2, 4)])


def spread(v):
    return v.reshape(32, 2, 4, 2, 4).transpose(0, 1, 3, 2, 4).reshape(32, 64)


def far_tables(partner, higher, lower, strengths, at):
    dy, slot = place(partner, at)
    near = jnp.where(dy == 0, slot, -1).astype(F32)
    table = jnp.concatenate([slot_of(higher, at), slot_of(lower, at)], axis=1).astype(F32)
    far = spread(pick(partner, table))
    slots = jnp.concatenate([far, near, jnp.full((32, 56), -1, F32)], axis=1)
    up, down = strengths[0, :4], strengths[0, 4:]
    products = [(a[:, None] * b[None, :]).reshape(16) for a in (up, down) for b in (up, down)]
    scale = jnp.concatenate([*products, up, down, jnp.zeros((56,), F32)]).reshape(1, DIM)
    return (slot >> 3) * EXTRA + dy * 16 + (slot & 7), slots, scale


def copies_of(blocks, held, sems, start, rows):
    return [
        pltpu.make_async_copy(b.at[pl.ds(start, rows), :], held.at[pl.ds(k * rows, rows), :], sems.at[k])
        for k, b in enumerate(blocks)
    ]


def link_sum(held, slots, weights, base, count):
    def add(k, total):
        for n in (base + 2 * k, base + 2 * k + 1):
            start = pl.multiple_of(slots[n] * ROWS, ROWS)
            total = total + weights[n] * held[pl.ds(start, ROWS), :].astype(F32)
        return total

    return lax.fori_loop(0, (count + 1) >> 1, add, jnp.zeros((ROWS, DIM), F32))


def mm(a, b):
    return jnp.dot(a, b, preferred_element_type=F32)


def crossed(plus):
    return jnp.concatenate([plus[DIM:], -plus[:DIM]], axis=1)


def near_sums(order, held, count, slots, weights, c_ref, outs, lefts, rights):
    for dy, out in zip(order, outs):

        def links(i, _):
            d = (dy * OWN + i) * 2
            up = link_sum(held, slots, weights, d * 4, count[d])
            down = link_sum(held, slots, weights, d * 4 + 4, count[d + 1])
            lefts[i] = crossed((up + down).astype(BF))
            rights[i] = (up - down).astype(BF)
            return 0

        lax.fori_loop(0, OWN, links, 0)
        c = c_ref[...]
        for i in range(OWN):
            left, right = mm(c, lefts[i]), mm(rights[i], c)
            out[pl.ds(i * ROWS, DIM), :] = (left[:, :DIM] - right[DIM:]).astype(out.dtype)
            out[pl.ds(i * ROWS + DIM, DIM), :] = (left[:, DIM:] + right[:DIM]).astype(out.dtype)


def near_kernel(order, count, slots, weights, c_ref, *refs):
    blocks, outs = refs[:32], refs[32 : 32 + len(order)]
    held, sems, lefts, rights = refs[32 + len(order) :]
    copies = copies_of(blocks, held, sems, 0, BLOCK)
    for copy in copies:
        copy.start()
    for copy in copies:
        copy.wait()
    near_sums(order, held, count, slots, weights, c_ref, outs, lefts, rights)


def make_lists(row_ref, ladder_ref, scale_ref, slot_ref, table, code_v, weight_v):
    lane = lax.broadcasted_iota(jnp.int32, (32, DIM), 1)
    row = lax.broadcasted_iota(jnp.int32, (DIM, DIM), 0)
    col = lax.broadcasted_iota(jnp.int32, (DIM, DIM), 1)
    wide = lax.broadcasted_iota(jnp.int32, (32, 32 * EXTRA), 1)
    total = jnp.zeros((32, DIM), F32)
    for k in range(2 * MODES):
        hot = jnp.where(row_ref[:, k : k + 1] == wide, 1.0, 0.0).astype(BF)
        wanted = mm(hot, table[...])
        mine = ladder_ref[:, k : k + 1]
        target = ((k // 4) * 2 + (row >> 2)) * 16 + (k % 4) * 4 + (row & 3)
        shift = jnp.where((row < 2 * MODES) & (col == target), 1.0, 0.0).astype(BF)
        total = total + mm((wanted * mine).astype(BF), shift)
        decay = wanted[:, 8:9] + wanted[:, 9:10] + wanted[:, 10:11]
        total = jnp.where(lane == 64 + k, decay * mine, total)
    slot = slot_ref[...]
    keep = (slot >= 0) & (total != 0)
    kept = jnp.where(keep, 1.0, 0.0)
    spot = mm(kept.astype(BF), jnp.where(row < col, 1.0, 0.0).astype(BF)).astype(jnp.int32)
    spot = jnp.where(keep, spot, -1)
    kind = jnp.where(lane < 64, lane >> 4, 4 + ((lane - 64) >> 2)).astype(F32)
    code, weight = slot + 256.0 * kind, total * scale_ref[...]
    codes = jnp.where(lane == DIM - 1, jnp.sum(kept, axis=1, keepdims=True), 0.0)
    weights = jnp.zeros((32, DIM), F32)
    for n in range(72):
        here = spot == n
        codes = jnp.where(lane == n, jnp.sum(jnp.where(here, code, 0.0), axis=1, keepdims=True), codes)
        weights = jnp.where(lane == n, jnp.sum(jnp.where(here, weight, 0.0), axis=1, keepdims=True), weights)
    code_v[...] = codes.astype(jnp.int32)
    weight_v[...] = weights


def far_kernel(order, c_ref, right_ref, left_ref, row_ref, ladder_ref, scale_ref, slot_ref, *refs):
    blocks, outs = refs[:32], refs[32 : 32 + len(order)]
    held, extra, main_sems, extra_sems, *rest = refs[32 + len(order) :]
    acc, lefts, rights, kept, double, code_v, weight_v, code_s, weight_s, sems = rest
    tails = copies_of(blocks, extra, extra_sems, BLOCK, EXTRA)
    mains = copies_of(blocks, held, main_sems, 0, BLOCK)
    for copy in tails + mains:
        copy.start()
    for copy in tails:
        copy.wait()
    make_lists(row_ref, ladder_ref, scale_ref, slot_ref, extra, code_v, weight_v)
    codes = pltpu.make_async_copy(code_v, code_s, sems.at[0])
    weights = pltpu.make_async_copy(weight_v, weight_s, sems.at[1])
    codes.start()
    weights.start()
    c = c_ref[...]
    double[0:DIM, 0:DIM] = c
    double[0:DIM, DIM:ROWS] = c
    double[DIM:ROWS, 0:DIM] = c
    double[DIM:ROWS, DIM:ROWS] = -c
    codes.wait()
    weights.wait()
    for copy in mains:
        copy.wait()
    for dy, out in zip(order, outs):

        def group(h, _):
            def links(g, _):
                d = dy * OWN + h * GROUP + g
                for k in range(6):
                    acc[k] = jnp.zeros((ROWS, DIM), F32)

                def add(e, _):
                    for n in (2 * e, 2 * e + 1):
                        code, weight = code_s[d, n], weight_s[d, n]
                        start = pl.multiple_of((code & 255) * ROWS, ROWS)
                        kind = code >> 8
                        acc[kind] = acc[kind] + weight * held[pl.ds(start, ROWS), :].astype(F32)
                    return 0

                lax.fori_loop(0, (code_s[d, DIM - 1] + 1) >> 1, add, 0)
                kept[g, 0] = acc[4] + acc[5]
                kept[g, 1] = acc[4] - acc[5]
                lefts[g, 0:DIM] = crossed((acc[0] + acc[1]).astype(BF))
                lefts[g, DIM:ROWS] = crossed((acc[2] + acc[3]).astype(BF))
                rights[g, :, 0:DIM] = (acc[0] - acc[1]).astype(BF)
                rights[g, :, DIM:ROWS] = (acc[2] - acc[3]).astype(BF)
                return 0

            lax.fori_loop(0, GROUP, links, 0)
            c, cc, w, wh = c_ref[...], double[...], right_ref[...], left_ref[...]
            turned = []
            for g in range(GROUP):
                left, right = mm(cc, lefts[g]), mm(rights[g], cc)
                halves = []
                for k in range(2):
                    side, cols = left[k * DIM : (k + 1) * DIM], right[:, k * DIM : (k + 1) * DIM]
                    re = kept[g, k, 0:DIM] + side[:, :DIM] - cols[DIM:]
                    im = kept[g, k, DIM:ROWS] + side[:, DIM:] + cols[:DIM]
                    halves.append(jnp.concatenate([re, im], axis=1).astype(BF))
                mid = mm(jnp.concatenate(halves), w).astype(BF)
                turned.append(mm(wh, stack_parts(mid)).astype(BF))
            for g in range(GROUP):
                left, right = mm(c, crossed(turned[g][:, :DIM])), mm(turned[g][:, DIM:], c)
                at = pl.multiple_of((h * GROUP + g) * ROWS, ROWS)
                out[pl.ds(at, DIM), :] = (left[:, :DIM] - right[DIM:]).astype(out.dtype)
                out[pl.ds(at + DIM, DIM), :] = (left[:, DIM:] + right[:DIM]).astype(out.dtype)
            return 0

        lax.fori_loop(0, OWN // GROUP, group, 0)


def stack_parts(mid):
    return jnp.concatenate(
        [
            jnp.concatenate([mid[:DIM, :DIM], mid[DIM:, :DIM]], axis=1),
            jnp.concatenate([mid[:DIM, DIM:], mid[DIM:, DIM:]], axis=1),
        ]
    )


SM = pl.BlockSpec(memory_space=pltpu.SMEM)
VM = pl.BlockSpec(memory_space=pltpu.VMEM)
FAR = pl.BlockSpec(memory_space=pltpu.HBM)


def part_shapes(order):
    return [jax.ShapeDtypeStruct((BLOCK, DIM), BF if dy else F32) for dy in order]


def near_scratch():
    return [pltpu.VMEM((OWN, DIM, ROWS), BF), pltpu.VMEM((OWN, ROWS, DIM), BF)]


def near_parts(order, lists, coupling, blocks):
    return pl.pallas_call(
        functools.partial(near_kernel, order),
        out_shape=part_shapes(order),
        in_specs=[SM] * 3 + [VM] + [FAR] * 32,
        out_specs=[VM] * len(order),
        scratch_shapes=[pltpu.VMEM((32 * BLOCK, DIM), BF), pltpu.SemaphoreType.DMA((32,))] + near_scratch(),
        compiler_params=pltpu.CompilerParams(vmem_limit_bytes=26 << 20),
        cost_estimate=pl.CostEstimate(flops=10**8, bytes_accessed=1 << 20, transcendentals=0),
    )(*lists, coupling, *blocks)


def far_parts(order, arrays, blocks):
    return pl.pallas_call(
        functools.partial(far_kernel, order),
        out_shape=part_shapes(order),
        in_specs=[VM] * len(arrays) + [FAR] * 32,
        out_specs=[VM] * len(order),
        scratch_shapes=[
            pltpu.VMEM((32 * BLOCK, DIM), BF),
            pltpu.VMEM((32 * EXTRA, DIM), BF),
            pltpu.SemaphoreType.DMA((32,)),
            pltpu.SemaphoreType.DMA((32,)),
            pltpu.VMEM((6, ROWS, DIM), F32),
            pltpu.VMEM((GROUP, ROWS, ROWS), BF),
            pltpu.VMEM((GROUP, ROWS, ROWS), BF),
            pltpu.VMEM((GROUP, 2, ROWS, DIM), F32),
            pltpu.VMEM((ROWS, ROWS), BF),
            pltpu.VMEM((32, DIM), jnp.int32),
            pltpu.VMEM((32, DIM), F32),
            pltpu.SMEM((32, DIM), jnp.int32),
            pltpu.SMEM((32, DIM), F32),
            pltpu.SemaphoreType.DMA((2,)),
        ],
        compiler_params=pltpu.CompilerParams(vmem_limit_bytes=30 << 20),
        cost_estimate=pl.CostEstimate(flops=10**8, bytes_accessed=1 << 20, transcendentals=0),
    )(*arrays, *blocks)


def chain_kernel(step, decay, lam_ref, own_ref, a_ref, b_ref, d_ref, right_ref, left_ref, saved_hbm, *refs):
    out_ref, grad_ref, wide, tall, saved_ref, sems = refs

    def saved_copy(u):
        return pltpu.make_async_copy(saved_hbm.at[step * 4 + u], saved_ref.at[u], sems.at[u])

    for u in range(4):
        saved_copy(u).start()
    for j in range(OWN):
        rows = pl.ds(j * ROWS, ROWS)
        mixed = decay[j] * lam_ref[rows, :].astype(F32) + own_ref[rows, :]
        mixed = mixed + a_ref[rows, :].astype(F32) + b_ref[rows, :].astype(F32) + d_ref[rows, :].astype(F32)
        mixed = mixed.astype(BF)
        wide[pl.ds(j * DIM, DIM), 0:DIM] = mixed[:DIM]
        wide[pl.ds(j * DIM, DIM), DIM:ROWS] = mixed[DIM:]

    def substep(u, _):
        right, left = right_ref[step * 4 + u], left_ref[step * 4 + u]
        for h in range(OWN // 2):
            mid = mm(wide[pl.ds(h * ROWS, ROWS), :], right).astype(BF)
            turned = mm(left, stack_parts(mid)).astype(BF)
            for k in range(2):
                re, im = turned[:DIM, k * DIM : (k + 1) * DIM], turned[DIM:, k * DIM : (k + 1) * DIM]
                j = 2 * h + k
                wide[pl.ds(j * DIM, DIM), 0:DIM] = re
                wide[pl.ds(j * DIM, DIM), DIM:ROWS] = im
                tall[pl.ds(j * ROWS, DIM), 0:DIM] = re
                tall[pl.ds(j * ROWS, DIM), DIM:ROWS] = im
                tall[pl.ds(j * ROWS + DIM, DIM), 0:DIM] = im
                tall[pl.ds(j * ROWS + DIM, DIM), DIM:ROWS] = -re
        saved_copy(u).wait()
        terms = lax.dot_general(
            saved_ref[u], tall[...], (((0,), (0,)), ((), ())), preferred_element_type=F32
        )
        grad_ref[u, 0] = terms[:, :DIM]
        grad_ref[u, 1] = terms[:, DIM:]
        return 0

    lax.fori_loop(0, 4, substep, 0)
    for j in range(OWN):
        out_ref[pl.ds(j * ROWS, DIM), :] = wide[pl.ds(j * DIM, DIM), 0:DIM]
        out_ref[pl.ds(j * ROWS + DIM, DIM), :] = wide[pl.ds(j * DIM, DIM), DIM:ROWS]


def chain(step, decay, lam, parts, right, left, saved):
    return pl.pallas_call(
        functools.partial(chain_kernel, step),
        out_shape=[
            jax.ShapeDtypeStruct((BLOCK, DIM), BF),
            jax.ShapeDtypeStruct((4, 2, DIM, DIM), F32),
        ],
        in_specs=[SM] + [VM] * 7 + [FAR],
        out_specs=[VM] * 2,
        scratch_shapes=[pltpu.VMEM((OWN * DIM, ROWS), BF), pltpu.VMEM((BLOCK, ROWS), BF), pltpu.VMEM((4, BLOCK, DIM), BF), pltpu.SemaphoreType.DMA((4,))],
        compiler_params=pltpu.CompilerParams(vmem_limit_bytes=8 << 20),
        cost_estimate=pl.CostEstimate(flops=10**8, bytes_accessed=1 << 20, transcendentals=0),
    )(decay, lam, *parts, right, left, saved)


def fill_right(out, re, im):
    out[0:DIM, 0:DIM] = re
    out[0:DIM, DIM:ROWS] = im
    out[DIM:ROWS, 0:DIM] = -im
    out[DIM:ROWS, DIM:ROWS] = re


def sides_kernel(prop_ref, whole_right, whole_left, right_ref, left_ref):
    for n in range(8):
        re, im = prop_ref[n, 0], prop_ref[n, 1]
        fill_right(right_ref.at[n], re, im)
        fill_right(left_ref.at[n], re.T, im.T)
    hi = lambda v: v.astype(BF)
    re, im = prop_ref[0, 0].astype(F32), prop_ref[0, 1].astype(F32)
    for u in range(1, 4):
        ur, ui = prop_ref[u, 0], prop_ref[u, 1]
        mul = lambda v, m: mm(hi(v), m) + mm(hi(v - hi(v).astype(F32)), m)
        re, im = mul(re, ur) - mul(im, ui), mul(re, ui) + mul(im, ur)
    fill_right(whole_right, hi(re), hi(im))
    fill_right(whole_left, hi(re.T), hi(im.T))


def sides(props):
    return pl.pallas_call(
        sides_kernel,
        out_shape=[jax.ShapeDtypeStruct((ROWS, ROWS), BF)] * 2 + [jax.ShapeDtypeStruct((8, ROWS, ROWS), BF)] * 2,
        in_specs=[VM],
        out_specs=[VM] * 4,
        compiler_params=pltpu.CompilerParams(vmem_limit_bytes=8 << 20),
    )(props)


def body(adjoint, saved, propagators, coupling, higher, lower, ladder, rates, decay):
    at = tuple(lax.axis_index(a) for a in AXES)
    lam = adjoint.reshape(BLOCK, DIM)
    meta = jnp.pad(own_meta(ladder, decay), ((0, 0), (0, 5)))
    by_y = [meta] + [send(meta, along_y(s)) for s in (1, 2, 3)]
    ladders = jnp.concatenate([by_y[(4 - dy) % 4][:, :8] for dy in range(4)])
    tail = jnp.pad(jnp.stack(by_y).astype(BF), ((0, 0), (0, 16 - OWN), (0, DIM - 16))).reshape(EXTRA, DIM)
    strengths = rates.reshape(1, 8)

    def prepare(arrived):
        tied = (propagators, higher, lower, ladders, strengths, arrived)
        props, up, down, wanted, factors, _ = lax.optimization_barrier(tied)
        partner = own_links(up, down, at)
        near = near_lists(partner, wanted * factors, at)
        return near, far_tables(partner, up, down, factors, at), sides(props.reshape(8, 2, DIM, DIM))

    made, blocks = gather_layer(jnp.concatenate([lam, tail]), prepare)
    one_list, (rows, slots, scale), (whole_right, whole_left, right, left) = made
    one_2, one_1, one_3, one_0 = near_parts((2, 1, 3, 0), one_list, coupling, blocks)
    got_one = [one_0] + [send(p, along_y(s)) for p, s in ((one_2, 2), (one_1, 1), (one_3, 3))]
    arrays = [coupling, whole_right, whole_left, rows, ladders, scale, slots]
    two_2, two_1, two_3 = far_parts((2, 1, 3), arrays, blocks)
    got_two = [send(p, along_y(s)) for p, s in ((two_2, 2), (two_1, 1), (two_3, 3))]
    [two_0] = far_parts((0,), arrays, blocks)
    got_two = [two_0] + got_two
    saved = saved.reshape(8, BLOCK, DIM)
    lam, grad_one = chain(0, decay, lam, got_one, right, left, saved)
    lam, grad_two = chain(1, decay, lam, got_two, right, left, saved)
    grad = jnp.concatenate([grad_one, grad_two]).astype(BF)
    grad = jnp.moveaxis(grad, 2, 0)
    grad = lax.all_to_all(grad, AXES, 0, 0, tiled=True)
    grad = jnp.sum(grad.astype(F32), axis=0, keepdims=True)
    return lam.reshape(OWN, 2, DIM, DIM), grad


def solution(mesh):
    finer = Mesh(mesh.devices.reshape(4, 2, 4, 4), AXES)
    rows = P(AXES)
    return jax.shard_map(
        body,
        mesh=finer,
        in_specs=(rows, P(None, None, AXES), P(), P(), P(), P(), P(None, AXES), P(), rows),
        out_specs=(rows, rows),
        check_vma=False,
    )
```

```python
import functools

import jax
import jax.numpy as jnp
import numpy as np
from jax import lax
from jax.experimental import pallas as pl
from jax.experimental.pallas import tpu as pltpu
from jax.sharding import Mesh
from jax.sharding import PartitionSpec as P

AXES = ("y", "c", "z", "x")
BF = jnp.bfloat16
F32 = jnp.float32
OWN = 8
MODES = 4
DIM = 128
ROWS = 2 * DIM
BLOCK = OWN * ROWS
GROUP = 4
EXTRA = 64


def pairs(move):
    out = []
    for y in range(4):
        for c in range(2):
            for z in range(4):
                for x in range(4):
                    ny, nc, nz, nx = move(y, c, z, x)
                    here = ((y * 2 + c) * 4 + z) * 4 + x
                    there = ((ny * 2 + nc) * 4 + nz) * 4 + nx
                    out.append((here, there))
    return out


def first(s):
    return pairs(lambda y, c, z, x: (y, c, z, (x + s) % 4) if c == 0 else (y, c, (z + s) % 4, x))


def second(s):
    return pairs(lambda y, c, z, x: (y, c, (z + s) % 4, x) if c == 0 else (y, c, z, (x + s) % 4))


def along_y(s):
    return pairs(lambda y, c, z, x: ((y + s) % 4, c, z, x))


SIBLING = pairs(lambda y, c, z, x: (y, 1 - c, z, x))


def send(a, route):
    return lax.ppermute(a, AXES, route)


def gather_layer(block, prepare):
    near = {0: block}
    for s in (1, 3, 2):
        near[s] = send(block, first(s))
    held = {(0, 0): block}
    twins = {(0, 0): send(block, SIBLING)}
    held[0, 1], held[0, 3] = send(block, second(1)), send(block, second(3))
    made = prepare(twins[0, 0])
    near[1], made = lax.optimization_barrier((near[1], made))
    for s in (1, 3, 2):
        held[s, 0] = near[s]
        held[s, 1] = send(near[s], second(1))
        held[s, 3] = send(near[s], second(3))
    for s, t in ((0, 1), (1, 3), (3, 1), (2, 3)):
        held[s, 2] = send(held[s, t], second(t))
    for key, value in held.items():
        if key not in twins:
            twins[key] = send(value, SIBLING)
    spots = [(s, t) for s in range(4) for t in range(4)]
    return made, [held[k] for k in spots] + [twins[k] for k in spots]


def own_meta(ladder, decay):
    top = lax.reduce_precision(decay, 8, 7)
    mid = lax.reduce_precision(decay - top, 8, 7)
    parts = [ladder[0].astype(F32), ladder[1].astype(F32), jnp.stack([top, mid, decay - top - mid], axis=1)]
    return jnp.concatenate(parts, axis=1)


def place(q, at):
    y, c, z, x = at
    owner = q >> 3
    oy, oc, oz, ox = owner >> 5, (owner >> 4) & 1, (owner >> 2) & 3, owner & 3
    dx, dz = (x - ox) & 3, (z - oz) & 3
    s = jnp.where(oc == 0, dx, dz)
    t = jnp.where(oc == 0, dz, dx)
    other = (oc != c).astype(jnp.int32)
    return (y - oy) & 3, ((other * 16 + s * 4 + t) << 3) + (q & 7)


def slot_of(q, at):
    dy, slot = place(q, at)
    return jnp.where(dy == 0, slot, -1)


def own_links(higher, lower, at):
    y, c, z, x = at
    rows = []
    for dy in range(4):
        start = ((((y + dy) & 3) * 2 + c) * 16 + z * 4 + x) * OWN
        both = [lax.dynamic_slice_in_dim(t, start, OWN, 0) for t in (higher, lower)]
        rows.append(jnp.concatenate(both, axis=1))
    return jnp.concatenate(rows)


def tables_of(higher, lower, at):
    partner = own_links(higher, lower, at)
    dy, slot = place(partner, at)
    table = jnp.concatenate([slot_of(higher, at), slot_of(lower, at)], axis=1).astype(BF)
    rows = (slot >> 3) * EXTRA + dy * 16 + (slot & 7)
    return partner, rows, jnp.where(dy == 0, slot, -1), table


def link_scale(rates):
    lane = np.arange(DIM)
    kind, near, far = lane >> 4, lane - 64, lane < 64
    outer = np.where(far, (kind >> 1) * 4 + ((lane >> 2) & 3), near)
    inner = np.where(far, (kind & 1) * 4 + (lane & 3), -1)
    eight = rates.reshape(1, 8)
    take = lambda n: jnp.sum(jnp.where(n[:, None] == np.arange(8)[None, :], eight, 0.0), axis=1)
    return (take(outer) * jnp.where(far, take(inner), 1.0)).reshape(1, DIM)


def copies_of(blocks, held, sems, start, rows):
    return [
        pltpu.make_async_copy(b.at[pl.ds(start, rows), :], held.at[pl.ds(k * rows, rows), :], sems.at[k])
        for k, b in enumerate(blocks)
    ]


def mm(a, b):
    return jnp.dot(a, b, preferred_element_type=F32)


def crossed(plus):
    return jnp.concatenate([plus[DIM:], -plus[:DIM]], axis=1)


def near_sums(order, held, slots, weights, c_ref, outs, acc, lefts, rights):
    for dy, out in zip(order, outs):

        def links(i, _):
            d = dy * OWN + i
            acc[...] = jnp.zeros((2, ROWS, DIM), F32)
            for k in range(2 * MODES):
                slot = slots[d, k]

                @pl.when(slot >= 0)
                def _():
                    start = pl.multiple_of(slot * ROWS, ROWS)
                    acc[k // 4] = acc[k // 4] + weights[d, k] * held[pl.ds(start, ROWS), :].astype(F32)

            lefts[i] = crossed((acc[0] + acc[1]).astype(BF))
            rights[i] = (acc[0] - acc[1]).astype(BF)
            return 0

        lax.fori_loop(0, OWN, links, 0)
        c = c_ref[...]
        for i in range(OWN):
            left, right = mm(c, lefts[i]), mm(rights[i], c)
            out[pl.ds(i * ROWS, DIM), :] = (left[:, :DIM] - right[DIM:]).astype(out.dtype)
            out[pl.ds(i * ROWS + DIM, DIM), :] = (left[:, DIM:] + right[:DIM]).astype(out.dtype)


def near_kernel(order, slots, weights, c_ref, *refs):
    blocks, outs = refs[:32], refs[32 : 32 + len(order)]
    held, sems, acc, lefts, rights = refs[32 + len(order) :]
    copies = copies_of(blocks, held, sems, 0, BLOCK)
    for copy in copies:
        copy.start()
    for copy in copies:
        copy.wait()
    near_sums(order, held, slots, weights, c_ref, outs, acc, lefts, rights)


def make_lists(partner_ref, row_ref, ladder_ref, scale_ref, slot_ref, links, table, code_v, weight_v):
    lane = lax.broadcasted_iota(jnp.int32, (32, DIM), 1)
    row = lax.broadcasted_iota(jnp.int32, (DIM, DIM), 0)
    col = lax.broadcasted_iota(jnp.int32, (DIM, DIM), 1)
    wide = lax.broadcasted_iota(jnp.int32, (32, 32 * EXTRA), 1)
    index = lax.broadcasted_iota(jnp.int32, (32, links.shape[0]), 1)
    total = jnp.zeros((32, DIM), F32)
    slot = jnp.zeros((32, DIM), F32)
    for k in range(2 * MODES):
        hot = jnp.where(row_ref[:, k : k + 1] == wide, 1.0, 0.0).astype(BF)
        wanted = mm(hot, table[...])
        mine = ladder_ref[:, k : k + 1]
        target = ((k // 4) * 2 + (row >> 2)) * 16 + (k % 4) * 4 + (row & 3)
        shift = jnp.where((row < 2 * MODES) & (col == target), 1.0, 0.0).astype(BF)
        total = total + mm((wanted * mine).astype(BF), shift)
        found = jnp.where(partner_ref[:, k : k + 1] == index, 1.0, 0.0).astype(BF)
        slot = slot + mm(mm(found, links[...]).astype(BF), shift[: 2 * MODES])
        slot = jnp.where(lane == 64 + k, slot_ref[:, k : k + 1].astype(F32), slot)
        decay = wanted[:, 8:9] + wanted[:, 9:10] + wanted[:, 10:11]
        total = jnp.where(lane == 64 + k, decay * mine, total)
    keep = (lane < 72) & (slot >= 0) & (total != 0)
    kept = jnp.where(keep, 1.0, 0.0)
    spot = mm(kept.astype(BF), jnp.where(row < col, 1.0, 0.0).astype(BF)).astype(jnp.int32)
    spot = jnp.where(keep, spot, -1)
    kind = jnp.where(lane < 64, lane >> 4, 4 + ((lane - 64) >> 2)).astype(F32)
    code, weight = slot + 256.0 * kind, total * scale_ref[...]
    codes = jnp.where(lane == DIM - 1, jnp.sum(kept, axis=1, keepdims=True), 0.0)
    weights = jnp.zeros((32, DIM), F32)
    for n in range(72):
        here = spot == n
        codes = jnp.where(lane == n, jnp.sum(jnp.where(here, code, 0.0), axis=1, keepdims=True), codes)
        weights = jnp.where(lane == n, jnp.sum(jnp.where(here, weight, 0.0), axis=1, keepdims=True), weights)
    code_v[...] = codes.astype(jnp.int32)
    weight_v[...] = weights


def far_kernel(order, c_ref, right_ref, left_ref, partner_ref, row_ref, ladder_ref, scale_ref, slot_ref, links, *refs):
    blocks, outs = refs[:32], refs[32 : 32 + len(order)]
    held, extra, main_sems, extra_sems, *rest = refs[32 + len(order) :]
    acc, lefts, rights, kept, double, code_v, weight_v, code_s, weight_s, sems = rest
    tails = copies_of(blocks, extra, extra_sems, BLOCK, EXTRA)
    mains = copies_of(blocks, held, main_sems, 0, BLOCK)
    for copy in tails + mains:
        copy.start()
    for copy in tails:
        copy.wait()
    make_lists(partner_ref, row_ref, ladder_ref, scale_ref, slot_ref, links, extra, code_v, weight_v)
    codes = pltpu.make_async_copy(code_v, code_s, sems.at[0])
    weights = pltpu.make_async_copy(weight_v, weight_s, sems.at[1])
    codes.start()
    weights.start()
    c = c_ref[...]
    double[0:DIM, 0:DIM] = c
    double[0:DIM, DIM:ROWS] = c
    double[DIM:ROWS, 0:DIM] = c
    double[DIM:ROWS, DIM:ROWS] = -c
    codes.wait()
    weights.wait()
    for copy in mains:
        copy.wait()
    for dy, out in zip(order, outs):

        def group(h, _):
            def links(g, _):
                d = dy * OWN + h * GROUP + g
                for k in range(6):
                    acc[k] = jnp.zeros((ROWS, DIM), F32)

                def add(e, _):
                    for n in (2 * e, 2 * e + 1):
                        code, weight = code_s[d, n], weight_s[d, n]
                        start = pl.multiple_of((code & 255) * ROWS, ROWS)
                        kind = code >> 8
                        acc[kind] = acc[kind] + weight * held[pl.ds(start, ROWS), :].astype(F32)
                    return 0

                lax.fori_loop(0, (code_s[d, DIM - 1] + 1) >> 1, add, 0)
                kept[g, 0] = acc[4] + acc[5]
                kept[g, 1] = acc[4] - acc[5]
                lefts[g, 0:DIM] = crossed((acc[0] + acc[1]).astype(BF))
                lefts[g, DIM:ROWS] = crossed((acc[2] + acc[3]).astype(BF))
                rights[g, :, 0:DIM] = (acc[0] - acc[1]).astype(BF)
                rights[g, :, DIM:ROWS] = (acc[2] - acc[3]).astype(BF)
                return 0

            lax.fori_loop(0, GROUP, links, 0)
            c, cc, w, wh = c_ref[...], double[...], right_ref[...], left_ref[...]
            turned = []
            for g in range(GROUP):
                left, right = mm(cc, lefts[g]), mm(rights[g], cc)
                halves = []
                for k in range(2):
                    side, cols = left[k * DIM : (k + 1) * DIM], right[:, k * DIM : (k + 1) * DIM]
                    re = kept[g, k, 0:DIM] + side[:, :DIM] - cols[DIM:]
                    im = kept[g, k, DIM:ROWS] + side[:, DIM:] + cols[:DIM]
                    halves.append(jnp.concatenate([re, im], axis=1).astype(BF))
                mid = mm(jnp.concatenate(halves), w).astype(BF)
                turned.append(mm(wh, stack_parts(mid)).astype(BF))
            for g in range(GROUP):
                left, right = mm(c, crossed(turned[g][:, :DIM])), mm(turned[g][:, DIM:], c)
                at = pl.multiple_of((h * GROUP + g) * ROWS, ROWS)
                out[pl.ds(at, DIM), :] = (left[:, :DIM] - right[DIM:]).astype(out.dtype)
                out[pl.ds(at + DIM, DIM), :] = (left[:, DIM:] + right[:DIM]).astype(out.dtype)
            return 0

        lax.fori_loop(0, OWN // GROUP, group, 0)


def stack_parts(mid):
    return jnp.concatenate(
        [
            jnp.concatenate([mid[:DIM, :DIM], mid[DIM:, :DIM]], axis=1),
            jnp.concatenate([mid[:DIM, DIM:], mid[DIM:, DIM:]], axis=1),
        ]
    )


SM = pl.BlockSpec(memory_space=pltpu.SMEM)
VM = pl.BlockSpec(memory_space=pltpu.VMEM)
FAR = pl.BlockSpec(memory_space=pltpu.HBM)


def part_shapes(order):
    return [jax.ShapeDtypeStruct((BLOCK, DIM), BF if dy else F32) for dy in order]


def near_scratch():
    return [pltpu.VMEM((2, ROWS, DIM), F32), pltpu.VMEM((OWN, DIM, ROWS), BF), pltpu.VMEM((OWN, ROWS, DIM), BF)]


def near_parts(order, lists, coupling, blocks):
    return pl.pallas_call(
        functools.partial(near_kernel, order),
        out_shape=part_shapes(order),
        in_specs=[SM] * 2 + [VM] + [FAR] * 32,
        out_specs=[VM] * len(order),
        scratch_shapes=[pltpu.VMEM((32 * BLOCK, DIM), BF), pltpu.SemaphoreType.DMA((32,))] + near_scratch(),
        compiler_params=pltpu.CompilerParams(vmem_limit_bytes=26 << 20),
        cost_estimate=pl.CostEstimate(flops=10**8, bytes_accessed=1 << 20, transcendentals=0),
    )(*lists, coupling, *blocks)


def far_parts(order, arrays, blocks):
    return pl.pallas_call(
        functools.partial(far_kernel, order),
        out_shape=part_shapes(order),
        in_specs=[VM] * len(arrays) + [FAR] * 32,
        out_specs=[VM] * len(order),
        scratch_shapes=[
            pltpu.VMEM((32 * BLOCK, DIM), BF),
            pltpu.VMEM((32 * EXTRA, DIM), BF),
            pltpu.SemaphoreType.DMA((32,)),
            pltpu.SemaphoreType.DMA((32,)),
            pltpu.VMEM((6, ROWS, DIM), F32),
            pltpu.VMEM((GROUP, ROWS, ROWS), BF),
            pltpu.VMEM((GROUP, ROWS, ROWS), BF),
            pltpu.VMEM((GROUP, 2, ROWS, DIM), F32),
            pltpu.VMEM((ROWS, ROWS), BF),
            pltpu.VMEM((32, DIM), jnp.int32),
            pltpu.VMEM((32, DIM), F32),
            pltpu.SMEM((32, DIM), jnp.int32),
            pltpu.SMEM((32, DIM), F32),
            pltpu.SemaphoreType.DMA((2,)),
        ],
        compiler_params=pltpu.CompilerParams(vmem_limit_bytes=30 << 20),
        cost_estimate=pl.CostEstimate(flops=10**8, bytes_accessed=1 << 20, transcendentals=0),
    )(*arrays, *blocks)


def chain_kernel(step, decay, lam_ref, own_ref, a_ref, b_ref, d_ref, right_ref, left_ref, saved_hbm, *refs):
    out_ref, grad_ref, wide, tall, saved_ref, sems = refs

    def saved_copy(u):
        return pltpu.make_async_copy(saved_hbm.at[step * 4 + u], saved_ref.at[u], sems.at[u])

    for u in range(4):
        saved_copy(u).start()
    for j in range(OWN):
        rows = pl.ds(j * ROWS, ROWS)
        mixed = decay[j] * lam_ref[rows, :].astype(F32) + own_ref[rows, :]
        mixed = mixed + a_ref[rows, :].astype(F32) + b_ref[rows, :].astype(F32) + d_ref[rows, :].astype(F32)
        mixed = mixed.astype(BF)
        wide[pl.ds(j * DIM, DIM), 0:DIM] = mixed[:DIM]
        wide[pl.ds(j * DIM, DIM), DIM:ROWS] = mixed[DIM:]

    def substep(u, _):
        right, left = right_ref[step * 4 + u], left_ref[step * 4 + u]
        for h in range(OWN // 2):
            mid = mm(wide[pl.ds(h * ROWS, ROWS), :], right).astype(BF)
            turned = mm(left, stack_parts(mid)).astype(BF)
            for k in range(2):
                re, im = turned[:DIM, k * DIM : (k + 1) * DIM], turned[DIM:, k * DIM : (k + 1) * DIM]
                j = 2 * h + k
                wide[pl.ds(j * DIM, DIM), 0:DIM] = re
                wide[pl.ds(j * DIM, DIM), DIM:ROWS] = im
                tall[pl.ds(j * ROWS, DIM), 0:DIM] = re
                tall[pl.ds(j * ROWS, DIM), DIM:ROWS] = im
                tall[pl.ds(j * ROWS + DIM, DIM), 0:DIM] = im
                tall[pl.ds(j * ROWS + DIM, DIM), DIM:ROWS] = -re
        saved_copy(u).wait()
        terms = lax.dot_general(
            saved_ref[u], tall[...], (((0,), (0,)), ((), ())), preferred_element_type=F32
        )
        grad_ref[u, 0] = terms[:, :DIM]
        grad_ref[u, 1] = terms[:, DIM:]
        return 0

    lax.fori_loop(0, 4, substep, 0)
    for j in range(OWN):
        out_ref[pl.ds(j * ROWS, DIM), :] = wide[pl.ds(j * DIM, DIM), 0:DIM]
        out_ref[pl.ds(j * ROWS + DIM, DIM), :] = wide[pl.ds(j * DIM, DIM), DIM:ROWS]


def chain(step, decay, lam, parts, right, left, saved):
    return pl.pallas_call(
        functools.partial(chain_kernel, step),
        out_shape=[
            jax.ShapeDtypeStruct((BLOCK, DIM), BF),
            jax.ShapeDtypeStruct((4, 2, DIM, DIM), F32),
        ],
        in_specs=[SM] + [VM] * 7 + [FAR],
        out_specs=[VM] * 2,
        scratch_shapes=[pltpu.VMEM((OWN * DIM, ROWS), BF), pltpu.VMEM((BLOCK, ROWS), BF), pltpu.VMEM((4, BLOCK, DIM), BF), pltpu.SemaphoreType.DMA((4,))],
        compiler_params=pltpu.CompilerParams(vmem_limit_bytes=8 << 20),
        cost_estimate=pl.CostEstimate(flops=10**8, bytes_accessed=1 << 20, transcendentals=0),
    )(decay, lam, *parts, right, left, saved)


def fill_right(out, re, im):
    out[0:DIM, 0:DIM] = re
    out[0:DIM, DIM:ROWS] = im
    out[DIM:ROWS, 0:DIM] = -im
    out[DIM:ROWS, DIM:ROWS] = re


def sides_kernel(prop_ref, *refs):
    small = (len(refs) - 4) // 2
    for given, out in zip(refs[:small], refs[small + 4 :]):
        out[...] = given[...]
    whole_right, whole_left, right_ref, left_ref = refs[small : small + 4]
    for n in range(8):
        re, im = prop_ref[n, 0], prop_ref[n, 1]
        fill_right(right_ref.at[n], re, im)
        fill_right(left_ref.at[n], re.T, im.T)
    hi = lambda v: v.astype(BF)
    re, im = prop_ref[0, 0].astype(F32), prop_ref[0, 1].astype(F32)
    for u in range(1, 4):
        ur, ui = prop_ref[u, 0], prop_ref[u, 1]
        mul = lambda v, m: mm(hi(v), m) + mm(hi(v - hi(v).astype(F32)), m)
        re, im = mul(re, ur) - mul(im, ui), mul(re, ui) + mul(im, ur)
    fill_right(whole_right, hi(re), hi(im))
    fill_right(whole_left, hi(re.T), hi(im.T))


def sides(props, small):
    return pl.pallas_call(
        sides_kernel,
        out_shape=[jax.ShapeDtypeStruct((ROWS, ROWS), BF)] * 2 + [jax.ShapeDtypeStruct((8, ROWS, ROWS), BF)] * 2
        + [jax.ShapeDtypeStruct(v.shape, v.dtype) for v in small],
        in_specs=[VM] * (1 + len(small)),
        out_specs=[VM] * (4 + len(small)),
        compiler_params=pltpu.CompilerParams(vmem_limit_bytes=8 << 20),
    )(props, *small)


def body(adjoint, saved, propagators, coupling, higher, lower, ladder, rates, decay):
    at = tuple(lax.axis_index(a) for a in AXES)
    lam = adjoint.reshape(BLOCK, DIM)
    meta = jnp.pad(own_meta(ladder, decay), ((0, 0), (0, 5)))
    by_y = [meta] + [send(meta, along_y(s)) for s in (1, 2, 3)]
    ladders = jnp.concatenate([by_y[(4 - dy) % 4][:, :8] for dy in range(4)])
    tail = jnp.pad(jnp.stack(by_y).astype(BF), ((0, 0), (0, 16 - OWN), (0, DIM - 16))).reshape(EXTRA, DIM)
    weights = ladders * rates.reshape(1, 8)
    scale = link_scale(rates)

    def prepare(arrived):
        tied = (propagators, higher, lower, weights, ladders, scale, arrived)
        props, up, down, *rest, _ = lax.optimization_barrier(tied)
        return sides(props.reshape(8, 2, DIM, DIM), [*rest, *tables_of(up, down, at)])

    made, blocks = gather_layer(jnp.concatenate([lam, tail]), prepare)
    whole_right, whole_left, right, left, weights, ladders, scale, partner, rows, slots, table = made
    one_2, one_1, one_3, one_0 = near_parts((2, 1, 3, 0), [slots, weights], coupling, blocks)
    got_one = [one_0] + [send(p, along_y(s)) for p, s in ((one_2, 2), (one_1, 1), (one_3, 3))]
    arrays = [coupling, whole_right, whole_left, partner, rows, ladders, scale, slots, table]
    two_2, two_1, two_3 = far_parts((2, 1, 3), arrays, blocks)
    got_two = [send(p, along_y(s)) for p, s in ((two_2, 2), (two_1, 1), (two_3, 3))]
    [two_0] = far_parts((0,), arrays, blocks)
    got_two = [two_0] + got_two
    saved = saved.reshape(8, BLOCK, DIM)
    lam, grad_one = chain(0, decay, lam, got_one, right, left, saved)
    lam, grad_two = chain(1, decay, lam, got_two, right, left, saved)
    grad = jnp.concatenate([grad_one, grad_two]).astype(BF)
    grad = jnp.moveaxis(grad, 2, 0)
    grad = lax.all_to_all(grad, AXES, 0, 0, tiled=True)
    grad = jnp.sum(grad.astype(F32), axis=0, keepdims=True)
    return lam.reshape(OWN, 2, DIM, DIM), grad


def solution(mesh):
    finer = Mesh(mesh.devices.reshape(4, 2, 4, 4), AXES)
    rows = P(AXES)
    return jax.shard_map(
        body,
        mesh=finer,
        in_specs=(rows, P(None, None, AXES), P(), P(), P(), P(), P(None, AXES), P(), rows),
        out_specs=(rows, rows),
        check_vma=False,
    )
```

```python
import functools

import jax
import jax.numpy as jnp
import numpy as np
from jax import lax
from jax.experimental import pallas as pl
from jax.experimental.pallas import tpu as pltpu
from jax.sharding import Mesh
from jax.sharding import PartitionSpec as P

AXES = ("y", "c", "z", "x")
BF = jnp.bfloat16
F32 = jnp.float32
OWN = 8
MODES = 4
DIM = 128
ROWS = 2 * DIM
BLOCK = OWN * ROWS
GROUP = 8
EXTRA = 64


def pairs(move):
    out = []
    for y in range(4):
        for c in range(2):
            for z in range(4):
                for x in range(4):
                    ny, nc, nz, nx = move(y, c, z, x)
                    here = ((y * 2 + c) * 4 + z) * 4 + x
                    there = ((ny * 2 + nc) * 4 + nz) * 4 + nx
                    out.append((here, there))
    return out


def first(s):
    return pairs(lambda y, c, z, x: (y, c, z, (x + s) % 4) if c == 0 else (y, c, (z + s) % 4, x))


def second(s):
    return pairs(lambda y, c, z, x: (y, c, (z + s) % 4, x) if c == 0 else (y, c, z, (x + s) % 4))


def along_y(s):
    return pairs(lambda y, c, z, x: ((y + s) % 4, c, z, x))


SIBLING = pairs(lambda y, c, z, x: (y, 1 - c, z, x))


def send(a, route):
    return lax.ppermute(a, AXES, route)


def gather_layer(block, prepare):
    near = {0: block}
    for s in (1, 3, 2):
        near[s] = send(block, first(s))
    held = {(0, 0): block}
    twins = {(0, 0): send(block, SIBLING)}
    held[0, 1], held[0, 3] = send(block, second(1)), send(block, second(3))
    made = prepare(twins[0, 0])
    near[1], made = lax.optimization_barrier((near[1], made))
    for s in (1, 3, 2):
        held[s, 0] = near[s]
        held[s, 1] = send(near[s], second(1))
        held[s, 3] = send(near[s], second(3))
    for s, t in ((0, 1), (1, 3), (3, 1), (2, 3)):
        held[s, 2] = send(held[s, t], second(t))
    for key, value in held.items():
        if key not in twins:
            twins[key] = send(value, SIBLING)
    spots = [(s, t) for s in range(4) for t in range(4)]
    return made, [held[k] for k in spots] + [twins[k] for k in spots]


def own_meta(ladder, decay):
    top = lax.reduce_precision(decay, 8, 7)
    mid = lax.reduce_precision(decay - top, 8, 7)
    parts = [ladder[0].astype(F32), ladder[1].astype(F32), jnp.stack([top, mid, decay - top - mid], axis=1)]
    return jnp.concatenate(parts, axis=1)


def place(q, at):
    y, c, z, x = at
    owner = q >> 3
    oy, oc, oz, ox = owner >> 5, (owner >> 4) & 1, (owner >> 2) & 3, owner & 3
    dx, dz = (x - ox) & 3, (z - oz) & 3
    s = jnp.where(oc == 0, dx, dz)
    t = jnp.where(oc == 0, dz, dx)
    other = (oc != c).astype(jnp.int32)
    return (y - oy) & 3, ((other * 16 + s * 4 + t) << 3) + (q & 7)


def slot_of(q, at):
    dy, slot = place(q, at)
    return jnp.where(dy == 0, slot, -1)


def own_links(higher, lower, at):
    y, c, z, x = at
    rows = []
    for dy in range(4):
        start = ((((y + dy) & 3) * 2 + c) * 16 + z * 4 + x) * OWN
        both = [lax.dynamic_slice_in_dim(t, start, OWN, 0) for t in (higher, lower)]
        rows.append(jnp.concatenate(both, axis=1))
    return jnp.concatenate(rows)


def tables_of(higher, lower, at):
    partner = own_links(higher, lower, at)
    dy, slot = place(partner, at)
    table = jnp.concatenate([slot_of(higher, at), slot_of(lower, at)], axis=1).astype(BF)
    rows = (slot >> 3) * EXTRA + dy * 16 + (slot & 7)
    return partner, rows, jnp.where(dy == 0, slot, -1), table


def link_scale(rates):
    lane = np.arange(DIM)
    kind, near, far = lane >> 4, lane - 64, lane < 64
    outer = np.where(far, (kind >> 1) * 4 + ((lane >> 2) & 3), near)
    inner = np.where(far, (kind & 1) * 4 + (lane & 3), -1)
    eight = rates.reshape(1, 8)
    take = lambda n: jnp.sum(jnp.where(n[:, None] == np.arange(8)[None, :], eight, 0.0), axis=1)
    return (take(outer) * jnp.where(far, take(inner), 1.0)).reshape(1, DIM)


def copies_of(blocks, held, sems, start, rows):
    return [
        pltpu.make_async_copy(b.at[pl.ds(start, rows), :], held.at[pl.ds(k * rows, rows), :], sems.at[k])
        for k, b in enumerate(blocks)
    ]


def mm(a, b):
    return jnp.dot(a, b, preferred_element_type=F32)


def crossed(plus):
    return jnp.concatenate([plus[DIM:], -plus[:DIM]], axis=1)


def near_sums(order, held, slots, weights, c_ref, outs, acc, lefts, rights):
    for dy, out in zip(order, outs):

        def links(i, _):
            d = dy * OWN + i
            acc[...] = jnp.zeros((2, ROWS, DIM), F32)
            for k in range(2 * MODES):
                slot = slots[d, k]

                @pl.when(slot >= 0)
                def _():
                    start = pl.multiple_of(slot * ROWS, ROWS)
                    acc[k // 4] = acc[k // 4] + weights[d, k] * held[pl.ds(start, ROWS), :].astype(F32)

            lefts[i] = crossed((acc[0] + acc[1]).astype(BF))
            rights[i] = (acc[0] - acc[1]).astype(BF)
            return 0

        lax.fori_loop(0, OWN, links, 0)
        c = c_ref[...]
        for i in range(OWN):
            left, right = mm(c, lefts[i]), mm(rights[i], c)
            out[pl.ds(i * ROWS, DIM), :] = (left[:, :DIM] - right[DIM:]).astype(out.dtype)
            out[pl.ds(i * ROWS + DIM, DIM), :] = (left[:, DIM:] + right[:DIM]).astype(out.dtype)


def near_kernel(order, slots, weights, c_ref, *refs):
    blocks, outs = refs[:32], refs[32 : 32 + len(order)]
    held, sems, acc, lefts, rights = refs[32 + len(order) :]
    copies = copies_of(blocks, held, sems, 0, BLOCK)
    for copy in copies:
        copy.start()
    for copy in copies:
        copy.wait()
    near_sums(order, held, slots, weights, c_ref, outs, acc, lefts, rights)


def make_lists(partner_ref, row_ref, ladder_ref, scale_ref, slot_ref, links, table, code_v, weight_v):
    lane = lax.broadcasted_iota(jnp.int32, (32, DIM), 1)
    row = lax.broadcasted_iota(jnp.int32, (DIM, DIM), 0)
    col = lax.broadcasted_iota(jnp.int32, (DIM, DIM), 1)
    wide = lax.broadcasted_iota(jnp.int32, (32, 32 * EXTRA), 1)
    index = lax.broadcasted_iota(jnp.int32, (32, links.shape[0]), 1)
    total = jnp.zeros((32, DIM), F32)
    slot = jnp.zeros((32, DIM), F32)
    for k in range(2 * MODES):
        hot = jnp.where(row_ref[:, k : k + 1] == wide, 1.0, 0.0).astype(BF)
        wanted = mm(hot, table[...])
        mine = ladder_ref[:, k : k + 1]
        target = ((k // 4) * 2 + (row >> 2)) * 16 + (k % 4) * 4 + (row & 3)
        shift = jnp.where((row < 2 * MODES) & (col == target), 1.0, 0.0).astype(BF)
        total = total + mm((wanted * mine).astype(BF), shift)
        found = jnp.where(partner_ref[:, k : k + 1] == index, 1.0, 0.0).astype(BF)
        slot = slot + mm(mm(found, links[...]).astype(BF), shift[: 2 * MODES])
        slot = jnp.where(lane == 64 + k, slot_ref[:, k : k + 1].astype(F32), slot)
        decay = wanted[:, 8:9] + wanted[:, 9:10] + wanted[:, 10:11]
        total = jnp.where(lane == 64 + k, decay * mine, total)
    keep = (lane < 72) & (slot >= 0) & (total != 0)
    kept = jnp.where(keep, 1.0, 0.0)
    spot = mm(kept.astype(BF), jnp.where(row < col, 1.0, 0.0).astype(BF)).astype(jnp.int32)
    spot = jnp.where(keep, spot, -1)
    kind = jnp.where(lane < 64, lane >> 4, 4 + ((lane - 64) >> 2)).astype(F32)
    code, weight = slot + 256.0 * kind, total * scale_ref[...]
    counts = jnp.sum(kept, axis=1, keepdims=True)

    def place_some(step, lists):
        codes, weights = lists
        for e in range(8):
            n = step * 8 + e
            here = spot == n
            one = jnp.sum(jnp.where(here, code, 0.0), axis=1, keepdims=True)
            two = jnp.sum(jnp.where(here, weight, 0.0), axis=1, keepdims=True)
            codes, weights = jnp.where(lane == n, one, codes), jnp.where(lane == n, two, weights)
        return codes, weights

    empty = (jnp.zeros((32, DIM), F32), jnp.zeros((32, DIM), F32))
    codes, weights = lax.fori_loop(0, (jnp.max(counts).astype(jnp.int32) + 7) >> 3, place_some, empty)
    codes = jnp.where(lane == DIM - 1, counts, codes)
    code_v[...] = codes.astype(jnp.int32)
    weight_v[...] = weights


def far_kernel(order, c_ref, right_ref, left_ref, *refs):
    small, blocks, refs = refs[:6], refs[6:38], refs[38:]
    outs, code_v, weight_v = refs[: len(order)], refs[len(order)], refs[len(order) + 1]
    held, main_sems, extra, extra_sems, *rest = refs[len(order) + 2 :]
    tails = copies_of(blocks, extra, extra_sems, BLOCK, EXTRA)
    mains = copies_of(blocks, held, main_sems, 0, BLOCK)
    for copy in tails + mains:
        copy.start()
    for copy in tails:
        copy.wait()
    make_lists(*small, extra, code_v, weight_v)
    far_sums(order, c_ref, right_ref, left_ref, outs, held, mains, code_v, weight_v, *rest)


def own_kernel(slots, weights, c_ref, right_ref, left_ref, code_v, weight_v, *refs):
    blocks, (far_out, near_out) = refs[:32], refs[32:34]
    held, main_sems, near_acc, near_lefts, near_rights, *rest = refs[34:]
    mains = copies_of(blocks, held, main_sems, 0, BLOCK)
    for copy in mains:
        copy.start()
    far_sums((0,), c_ref, right_ref, left_ref, (far_out,), held, mains, code_v, weight_v, *rest)
    near_sums((0,), held, slots, weights, c_ref, (near_out,), near_acc, near_lefts, near_rights)


def far_sums(order, c_ref, right_ref, left_ref, outs, held, mains, code_v, weight_v, *refs):
    acc, lefts, rights, kept, double, code_s, weight_s, sems = refs
    codes = pltpu.make_async_copy(code_v, code_s, sems.at[0])
    weights = pltpu.make_async_copy(weight_v, weight_s, sems.at[1])
    codes.start()
    weights.start()
    c = c_ref[...]
    double[0:DIM, 0:DIM] = c
    double[0:DIM, DIM:ROWS] = c
    double[DIM:ROWS, 0:DIM] = c
    double[DIM:ROWS, DIM:ROWS] = -c
    codes.wait()
    weights.wait()
    for copy in mains:
        copy.wait()
    for dy, out in zip(order, outs):

        def group(h, _):
            def links(g, _):
                d = dy * OWN + h * GROUP + g
                for k in range(6):
                    acc[k] = jnp.zeros((ROWS, DIM), F32)

                def add(e, _):
                    for n in (2 * e, 2 * e + 1):
                        code, weight = code_s[d, n], weight_s[d, n]
                        start = pl.multiple_of((code & 255) * ROWS, ROWS)
                        kind = code >> 8
                        acc[kind] = acc[kind] + weight * held[pl.ds(start, ROWS), :].astype(F32)
                    return 0

                lax.fori_loop(0, (code_s[d, DIM - 1] + 1) >> 1, add, 0)
                kept[g, 0] = acc[4] + acc[5]
                kept[g, 1] = acc[4] - acc[5]
                at = pl.multiple_of(g * ROWS, ROWS)
                lefts[0:DIM, pl.ds(at, ROWS)] = crossed((acc[0] + acc[1]).astype(BF))
                lefts[DIM:ROWS, pl.ds(at, ROWS)] = crossed((acc[2] + acc[3]).astype(BF))
                rights[pl.ds(at, ROWS), 0:DIM] = (acc[0] - acc[1]).astype(BF)
                rights[pl.ds(at, ROWS), DIM:ROWS] = (acc[2] - acc[3]).astype(BF)
                return 0

            lax.fori_loop(0, GROUP, links, 0)
            c, cc, w, wh = c_ref[...], double[...], right_ref[...], left_ref[...]
            cuts = [slice(g * ROWS, (g + 1) * ROWS) for g in range(GROUP)]
            left, right = mm(cc, lefts[...]), mm(rights[...], cc)
            halves = []
            for g, at in enumerate(cuts):
                for k in range(2):
                    side, cols = left[k * DIM : (k + 1) * DIM, at], right[at, k * DIM : (k + 1) * DIM]
                    re = kept[g, k, 0:DIM] + side[:, :DIM] - cols[DIM:]
                    im = kept[g, k, DIM:ROWS] + side[:, DIM:] + cols[:DIM]
                    halves.append(jnp.concatenate([re, im], axis=1).astype(BF))
            mid = mm(jnp.concatenate(halves), w).astype(BF)
            turned = mm(wh, jnp.concatenate([stack_parts(mid[at]) for at in cuts], axis=1)).astype(BF)
            parts = [turned[:, at] for at in cuts]
            left = mm(c, jnp.concatenate([crossed(t[:, :DIM]) for t in parts], axis=1))
            right = mm(jnp.concatenate([t[:, DIM:] for t in parts]), c)
            for g, at in enumerate(cuts):
                to = pl.multiple_of((h * GROUP + g) * ROWS, ROWS)
                out[pl.ds(to, DIM), :] = (left[:, at][:, :DIM] - right[at][DIM:]).astype(out.dtype)
                out[pl.ds(to + DIM, DIM), :] = (left[:, at][:, DIM:] + right[at][:DIM]).astype(out.dtype)
            return 0

        lax.fori_loop(0, OWN // GROUP, group, 0)


def stack_parts(mid):
    return jnp.concatenate(
        [
            jnp.concatenate([mid[:DIM, :DIM], mid[DIM:, :DIM]], axis=1),
            jnp.concatenate([mid[:DIM, DIM:], mid[DIM:, DIM:]], axis=1),
        ]
    )


SM = pl.BlockSpec(memory_space=pltpu.SMEM)
VM = pl.BlockSpec(memory_space=pltpu.VMEM)
FAR = pl.BlockSpec(memory_space=pltpu.HBM)


def part_shapes(order):
    return [jax.ShapeDtypeStruct((BLOCK, DIM), BF if dy else F32) for dy in order]


def near_scratch():
    return [pltpu.VMEM((2, ROWS, DIM), F32), pltpu.VMEM((OWN, DIM, ROWS), BF), pltpu.VMEM((OWN, ROWS, DIM), BF)]


def near_parts(order, lists, coupling, blocks):
    return pl.pallas_call(
        functools.partial(near_kernel, order),
        out_shape=part_shapes(order),
        in_specs=[SM] * 2 + [VM] + [FAR] * 32,
        out_specs=[VM] * len(order),
        scratch_shapes=[pltpu.VMEM((32 * BLOCK, DIM), BF), pltpu.SemaphoreType.DMA((32,))] + near_scratch(),
        compiler_params=pltpu.CompilerParams(vmem_limit_bytes=26 << 20),
        cost_estimate=pl.CostEstimate(flops=10**8, bytes_accessed=1 << 20, transcendentals=0),
    )(*lists, coupling, *blocks)


def far_scratch():
    return [
        pltpu.VMEM((6, ROWS, DIM), F32),
        pltpu.VMEM((ROWS, GROUP * ROWS), BF),
        pltpu.VMEM((GROUP * ROWS, ROWS), BF),
        pltpu.VMEM((GROUP, 2, ROWS, DIM), F32),
        pltpu.VMEM((ROWS, ROWS), BF),
        pltpu.SMEM((32, DIM), jnp.int32),
        pltpu.SMEM((32, DIM), F32),
        pltpu.SemaphoreType.DMA((2,)),
    ]


def held_scratch(rows):
    return [pltpu.VMEM((32 * rows, DIM), BF), pltpu.SemaphoreType.DMA((32,))]


LISTS = [jax.ShapeDtypeStruct((32, DIM), jnp.int32), jax.ShapeDtypeStruct((32, DIM), F32)]


def far_parts(order, arrays, blocks):
    return pl.pallas_call(
        functools.partial(far_kernel, order),
        out_shape=part_shapes(order) + LISTS,
        in_specs=[VM] * len(arrays) + [FAR] * 32,
        out_specs=[VM] * (len(order) + 2),
        scratch_shapes=held_scratch(BLOCK) + held_scratch(EXTRA) + far_scratch(),
        compiler_params=pltpu.CompilerParams(vmem_limit_bytes=30 << 20),
        cost_estimate=pl.CostEstimate(flops=10**8, bytes_accessed=1 << 20, transcendentals=0),
    )(*arrays, *blocks)


def own_parts(scalars, arrays, blocks):
    return pl.pallas_call(
        own_kernel,
        out_shape=part_shapes((0, 0)),
        in_specs=[SM] * 2 + [VM] * len(arrays) + [FAR] * 32,
        out_specs=[VM] * 2,
        scratch_shapes=held_scratch(BLOCK) + near_scratch() + far_scratch(),
        compiler_params=pltpu.CompilerParams(vmem_limit_bytes=30 << 20),
        cost_estimate=pl.CostEstimate(flops=10**8, bytes_accessed=1 << 20, transcendentals=0),
    )(*scalars, *arrays, *blocks)


def chain_kernel(step, decay, lam_ref, own_ref, a_ref, b_ref, d_ref, right_ref, left_ref, saved_hbm, *refs):
    out_ref, grad_ref, wide, tall, saved_ref, sems = refs

    def saved_copy(u):
        return pltpu.make_async_copy(saved_hbm.at[step * 4 + u], saved_ref.at[u], sems.at[u])

    for u in range(4):
        saved_copy(u).start()
    for j in range(OWN):
        rows = pl.ds(j * ROWS, ROWS)
        mixed = decay[j] * lam_ref[rows, :].astype(F32) + own_ref[rows, :]
        mixed = mixed + a_ref[rows, :].astype(F32) + b_ref[rows, :].astype(F32) + d_ref[rows, :].astype(F32)
        mixed = mixed.astype(BF)
        wide[pl.ds(j * DIM, DIM), 0:DIM] = mixed[:DIM]
        wide[pl.ds(j * DIM, DIM), DIM:ROWS] = mixed[DIM:]

    def substep(u, _):
        right, left = right_ref[step * 4 + u], left_ref[step * 4 + u]
        for h in range(OWN // 2):
            mid = mm(wide[pl.ds(h * ROWS, ROWS), :], right).astype(BF)
            turned = mm(left, stack_parts(mid)).astype(BF)
            for k in range(2):
                re, im = turned[:DIM, k * DIM : (k + 1) * DIM], turned[DIM:, k * DIM : (k + 1) * DIM]
                j = 2 * h + k
                wide[pl.ds(j * DIM, DIM), 0:DIM] = re
                wide[pl.ds(j * DIM, DIM), DIM:ROWS] = im
                tall[pl.ds(j * ROWS, DIM), 0:DIM] = re
                tall[pl.ds(j * ROWS, DIM), DIM:ROWS] = im
                tall[pl.ds(j * ROWS + DIM, DIM), 0:DIM] = im
                tall[pl.ds(j * ROWS + DIM, DIM), DIM:ROWS] = -re
        saved_copy(u).wait()
        terms = lax.dot_general(
            saved_ref[u], tall[...], (((0,), (0,)), ((), ())), preferred_element_type=F32
        )
        grad_ref[u, 0] = terms[:, :DIM]
        grad_ref[u, 1] = terms[:, DIM:]
        return 0

    lax.fori_loop(0, 4, substep, 0)
    for j in range(OWN):
        out_ref[pl.ds(j * ROWS, DIM), :] = wide[pl.ds(j * DIM, DIM), 0:DIM]
        out_ref[pl.ds(j * ROWS + DIM, DIM), :] = wide[pl.ds(j * DIM, DIM), DIM:ROWS]


def chain(step, decay, lam, parts, right, left, saved):
    return pl.pallas_call(
        functools.partial(chain_kernel, step),
        out_shape=[
            jax.ShapeDtypeStruct((BLOCK, DIM), BF),
            jax.ShapeDtypeStruct((4, 2, DIM, DIM), F32),
        ],
        in_specs=[SM] + [VM] * 7 + [FAR],
        out_specs=[VM] * 2,
        scratch_shapes=[pltpu.VMEM((OWN * DIM, ROWS), BF), pltpu.VMEM((BLOCK, ROWS), BF), pltpu.VMEM((4, BLOCK, DIM), BF), pltpu.SemaphoreType.DMA((4,))],
        compiler_params=pltpu.CompilerParams(vmem_limit_bytes=8 << 20),
        cost_estimate=pl.CostEstimate(flops=10**8, bytes_accessed=1 << 20, transcendentals=0),
    )(decay, lam, *parts, right, left, saved)


def fill_right(out, re, im):
    out[0:DIM, 0:DIM] = re
    out[0:DIM, DIM:ROWS] = im
    out[DIM:ROWS, 0:DIM] = -im
    out[DIM:ROWS, DIM:ROWS] = re


def sides_kernel(prop_ref, *refs):
    small = (len(refs) - 4) // 2
    for given, out in zip(refs[:small], refs[small + 4 :]):
        out[...] = given[...]
    whole_right, whole_left, right_ref, left_ref = refs[small : small + 4]
    for n in range(8):
        re, im = prop_ref[n, 0], prop_ref[n, 1]
        fill_right(right_ref.at[n], re, im)
        fill_right(left_ref.at[n], re.T, im.T)
    hi = lambda v: v.astype(BF)
    re, im = prop_ref[0, 0].astype(F32), prop_ref[0, 1].astype(F32)
    for u in range(1, 4):
        ur, ui = prop_ref[u, 0], prop_ref[u, 1]
        mul = lambda v, m: mm(hi(v), m) + mm(hi(v - hi(v).astype(F32)), m)
        re, im = mul(re, ur) - mul(im, ui), mul(re, ui) + mul(im, ur)
    fill_right(whole_right, hi(re), hi(im))
    fill_right(whole_left, hi(re.T), hi(im.T))


def sides(props, small):
    return pl.pallas_call(
        sides_kernel,
        out_shape=[jax.ShapeDtypeStruct((ROWS, ROWS), BF)] * 2 + [jax.ShapeDtypeStruct((8, ROWS, ROWS), BF)] * 2
        + [jax.ShapeDtypeStruct(v.shape, v.dtype) for v in small],
        in_specs=[VM] * (1 + len(small)),
        out_specs=[VM] * (4 + len(small)),
        compiler_params=pltpu.CompilerParams(vmem_limit_bytes=8 << 20),
    )(props, *small)


def body(adjoint, saved, propagators, coupling, higher, lower, ladder, rates, decay):
    at = tuple(lax.axis_index(a) for a in AXES)
    lam = adjoint.reshape(BLOCK, DIM)
    meta = jnp.pad(own_meta(ladder, decay), ((0, 0), (0, 5)))
    by_y = [meta] + [send(meta, along_y(s)) for s in (1, 2, 3)]
    ladders = jnp.concatenate([by_y[(4 - dy) % 4][:, :8] for dy in range(4)])
    tail = jnp.pad(jnp.stack(by_y).astype(BF), ((0, 0), (0, 16 - OWN), (0, DIM - 16))).reshape(EXTRA, DIM)
    weights = ladders * rates.reshape(1, 8)
    scale = link_scale(rates)

    def prepare(arrived):
        tied = (propagators, higher, lower, weights, ladders, scale, arrived)
        props, up, down, *rest, _ = lax.optimization_barrier(tied)
        return sides(props.reshape(8, 2, DIM, DIM), [*rest, *tables_of(up, down, at)])

    made, blocks = gather_layer(jnp.concatenate([lam, tail]), prepare)
    whole_right, whole_left, right, left, weights, ladders, scale, partner, rows, slots, table = made
    one_2, one_1, one_3 = near_parts((2, 1, 3), [slots, weights], coupling, blocks)
    got_one = [send(p, along_y(s)) for p, s in ((one_2, 2), (one_1, 1), (one_3, 3))]
    whole = [coupling, whole_right, whole_left]
    small = [partner, rows, ladders, scale, slots, table]
    two_2, two_1, two_3, *lists = far_parts((2, 1, 3), whole + small, blocks)
    got_two = [send(p, along_y(s)) for p, s in ((two_2, 2), (two_1, 1), (two_3, 3))]
    two_0, one_0 = own_parts([slots, weights], whole + lists, blocks)
    got_one, got_two = [one_0] + got_one, [two_0] + got_two
    saved = saved.reshape(8, BLOCK, DIM)
    lam, grad_one = chain(0, decay, lam, got_one, right, left, saved)
    lam, grad_two = chain(1, decay, lam, got_two, right, left, saved)
    grad = jnp.concatenate([grad_one, grad_two]).astype(BF)
    grad = jnp.moveaxis(grad, 2, 0)
    grad = lax.all_to_all(grad, AXES, 0, 0, tiled=True)
    grad = jnp.sum(grad.astype(F32), axis=0, keepdims=True)
    return lam.reshape(OWN, 2, DIM, DIM), grad


def solution(mesh):
    finer = Mesh(mesh.devices.reshape(4, 2, 4, 4), AXES)
    rows = P(AXES)
    return jax.shard_map(
        body,
        mesh=finer,
        in_specs=(rows, P(None, None, AXES), P(), P(), P(), P(), P(None, AXES), P(), rows),
        out_specs=(rows, rows),
        check_vma=False,
    )
```

```python
import functools

import jax
import jax.numpy as jnp
import numpy as np
from jax import lax
from jax.experimental import pallas as pl
from jax.experimental.pallas import tpu as pltpu
from jax.sharding import Mesh
from jax.sharding import PartitionSpec as P

AXES = ("y", "c", "z", "x")
BF = jnp.bfloat16
F32 = jnp.float32
OWN = 8
MODES = 4
DIM = 128
ROWS = 2 * DIM
BLOCK = OWN * ROWS
GROUP = 8
EXTRA = 64


def pairs(move):
    out = []
    for y in range(4):
        for c in range(2):
            for z in range(4):
                for x in range(4):
                    ny, nc, nz, nx = move(y, c, z, x)
                    here = ((y * 2 + c) * 4 + z) * 4 + x
                    there = ((ny * 2 + nc) * 4 + nz) * 4 + nx
                    out.append((here, there))
    return out


def first(s):
    return pairs(lambda y, c, z, x: (y, c, z, (x + s) % 4) if c == 0 else (y, c, (z + s) % 4, x))


def second(s):
    return pairs(lambda y, c, z, x: (y, c, (z + s) % 4, x) if c == 0 else (y, c, z, (x + s) % 4))


def along_y(s):
    return pairs(lambda y, c, z, x: ((y + s) % 4, c, z, x))


SIBLING = pairs(lambda y, c, z, x: (y, 1 - c, z, x))


def send(a, route):
    return lax.ppermute(a, AXES, route)


def gather_layer(block, prepare):
    near = {0: block}
    for s in (1, 3, 2):
        near[s] = send(block, first(s))
    held = {(0, 0): block}
    twins = {(0, 0): send(block, SIBLING)}
    held[0, 1], held[0, 3] = send(block, second(1)), send(block, second(3))
    made = prepare(twins[0, 0])
    near[1], made = lax.optimization_barrier((near[1], made))
    for s in (1, 3, 2):
        held[s, 0] = near[s]
        held[s, 1] = send(near[s], second(1))
        held[s, 3] = send(near[s], second(3))
    for s, t in ((0, 1), (1, 3), (3, 1), (2, 3)):
        held[s, 2] = send(held[s, t], second(t))
    for key, value in held.items():
        if key not in twins:
            twins[key] = send(value, SIBLING)
    spots = [(s, t) for s in range(4) for t in range(4)]
    return made, [held[k] for k in spots] + [twins[k] for k in spots]


def own_meta(ladder, decay):
    top = lax.reduce_precision(decay, 8, 7)
    mid = lax.reduce_precision(decay - top, 8, 7)
    parts = [ladder[0].astype(F32), ladder[1].astype(F32), jnp.stack([top, mid, decay - top - mid], axis=1)]
    return jnp.concatenate(parts, axis=1)


def place(q, at):
    y, c, z, x = at
    owner = q >> 3
    oy, oc, oz, ox = owner >> 5, (owner >> 4) & 1, (owner >> 2) & 3, owner & 3
    dx, dz = (x - ox) & 3, (z - oz) & 3
    s = jnp.where(oc == 0, dx, dz)
    t = jnp.where(oc == 0, dz, dx)
    other = (oc != c).astype(jnp.int32)
    return (y - oy) & 3, ((other * 16 + s * 4 + t) << 3) + (q & 7)


def slot_of(q, at):
    dy, slot = place(q, at)
    return jnp.where(dy == 0, slot, -1)


def own_links(higher, lower, at):
    y, c, z, x = at
    rows = []
    for dy in range(4):
        start = ((((y + dy) & 3) * 2 + c) * 16 + z * 4 + x) * OWN
        both = [lax.dynamic_slice_in_dim(t, start, OWN, 0) for t in (higher, lower)]
        rows.append(jnp.concatenate(both, axis=1))
    return jnp.concatenate(rows)


def tables_of(higher, lower, at):
    partner = own_links(higher, lower, at)
    dy, slot = place(partner, at)
    table = jnp.concatenate([slot_of(higher, at), slot_of(lower, at)], axis=1).astype(BF)
    rows = (slot >> 3) * EXTRA + dy * 16 + (slot & 7)
    return partner, rows, jnp.where(dy == 0, slot, -1), table


def link_scale(rates):
    lane = np.arange(DIM)
    kind, near, far = lane >> 4, lane - 64, lane < 64
    outer = np.where(far, (kind >> 1) * 4 + ((lane >> 2) & 3), near)
    inner = np.where(far, (kind & 1) * 4 + (lane & 3), -1)
    eight = rates.reshape(1, 8)
    take = lambda n: jnp.sum(jnp.where(n[:, None] == np.arange(8)[None, :], eight, 0.0), axis=1)
    return (take(outer) * jnp.where(far, take(inner), 1.0)).reshape(1, DIM)


def copies_of(blocks, held, sems, start, rows):
    return [
        pltpu.make_async_copy(b.at[pl.ds(start, rows), :], held.at[pl.ds(k * rows, rows), :], sems.at[k])
        for k, b in enumerate(blocks)
    ]


def mm(a, b):
    return jnp.dot(a, b, preferred_element_type=F32)


def crossed(plus):
    return jnp.concatenate([plus[DIM:], -plus[:DIM]], axis=1)


def near_sums(order, held, slots, weights, c_ref, outs, acc, lefts, rights):
    for dy, out in zip(order, outs):

        def links(i, _):
            d = dy * OWN + i
            acc[...] = jnp.zeros((2, ROWS, DIM), F32)
            for k in range(2 * MODES):
                slot = slots[d, k]

                @pl.when(slot >= 0)
                def _():
                    start = pl.multiple_of(slot * ROWS, ROWS)
                    acc[k // 4] = acc[k // 4] + weights[d, k] * held[pl.ds(start, ROWS), :].astype(F32)

            lefts[i] = crossed((acc[0] + acc[1]).astype(BF))
            rights[i] = (acc[0] - acc[1]).astype(BF)
            return 0

        lax.fori_loop(0, OWN, links, 0)
        c = c_ref[...]
        for i in range(OWN):
            left, right = mm(c, lefts[i]), mm(rights[i], c)
            out[pl.ds(i * ROWS, DIM), :] = (left[:, :DIM] - right[DIM:]).astype(out.dtype)
            out[pl.ds(i * ROWS + DIM, DIM), :] = (left[:, DIM:] + right[:DIM]).astype(out.dtype)


def near_kernel(order, slots, weights, c_ref, *refs):
    blocks, outs = refs[:32], refs[32 : 32 + len(order)]
    held, sems, acc, lefts, rights = refs[32 + len(order) :]
    copies = copies_of(blocks, held, sems, 0, BLOCK)
    for copy in copies:
        copy.start()
    for copy in copies:
        copy.wait()
    near_sums(order, held, slots, weights, c_ref, outs, acc, lefts, rights)


def make_lists(partner_ref, row_ref, ladder_ref, scale_ref, slot_ref, links, table, code_v, weight_v):
    lane = lax.broadcasted_iota(jnp.int32, (32, DIM), 1)
    row = lax.broadcasted_iota(jnp.int32, (DIM, DIM), 0)
    col = lax.broadcasted_iota(jnp.int32, (DIM, DIM), 1)
    wide = lax.broadcasted_iota(jnp.int32, (32, 32 * EXTRA), 1)
    index = lax.broadcasted_iota(jnp.int32, (32, links.shape[0]), 1)
    total = jnp.zeros((32, DIM), F32)
    slot = jnp.zeros((32, DIM), F32)
    for k in range(2 * MODES):
        hot = jnp.where(row_ref[:, k : k + 1] == wide, 1.0, 0.0).astype(BF)
        wanted = mm(hot, table[...])
        mine = ladder_ref[:, k : k + 1]
        target = ((k // 4) * 2 + (row >> 2)) * 16 + (k % 4) * 4 + (row & 3)
        shift = jnp.where((row < 2 * MODES) & (col == target), 1.0, 0.0).astype(BF)
        total = total + mm((wanted * mine).astype(BF), shift)
        found = jnp.where(partner_ref[:, k : k + 1] == index, 1.0, 0.0).astype(BF)
        slot = slot + mm(mm(found, links[...]).astype(BF), shift[: 2 * MODES])
        slot = jnp.where(lane == 64 + k, slot_ref[:, k : k + 1].astype(F32), slot)
        decay = wanted[:, 8:9] + wanted[:, 9:10] + wanted[:, 10:11]
        total = jnp.where(lane == 64 + k, decay * mine, total)
    keep = (lane < 72) & (slot >= 0) & (total != 0)
    kept = jnp.where(keep, 1.0, 0.0)
    spot = mm(kept.astype(BF), jnp.where(row < col, 1.0, 0.0).astype(BF)).astype(jnp.int32)
    spot = jnp.where(keep, spot, -1)
    kind = jnp.where(lane < 64, lane >> 4, 4 + ((lane - 64) >> 2)).astype(F32)
    code, weight = slot + 256.0 * kind, total * scale_ref[...]
    counts = jnp.sum(kept, axis=1, keepdims=True)

    def place_some(step, lists):
        codes, weights = lists
        for e in range(8):
            n = step * 8 + e
            here = spot == n
            one = jnp.sum(jnp.where(here, code, 0.0), axis=1, keepdims=True)
            two = jnp.sum(jnp.where(here, weight, 0.0), axis=1, keepdims=True)
            codes, weights = jnp.where(lane == n, one, codes), jnp.where(lane == n, two, weights)
        return codes, weights

    empty = (jnp.zeros((32, DIM), F32), jnp.zeros((32, DIM), F32))
    codes, weights = lax.fori_loop(0, (jnp.max(counts).astype(jnp.int32) + 7) >> 3, place_some, empty)
    codes = jnp.where(lane == DIM - 1, counts, codes)
    code_v[...] = codes.astype(jnp.int32)
    weight_v[...] = weights


def far_kernel(order, c_ref, right_ref, left_ref, *refs):
    small, blocks, refs = refs[:6], refs[6:38], refs[38:]
    outs, code_v, weight_v = refs[: len(order)], refs[len(order)], refs[len(order) + 1]
    held, main_sems, extra, extra_sems, *rest = refs[len(order) + 2 :]
    tails = copies_of(blocks, extra, extra_sems, BLOCK, EXTRA)
    mains = copies_of(blocks, held, main_sems, 0, BLOCK)
    for copy in tails + mains:
        copy.start()
    for copy in tails:
        copy.wait()
    make_lists(*small, extra, code_v, weight_v)
    far_sums(order, c_ref, right_ref, left_ref, outs, held, mains, code_v, weight_v, *rest)


def more_kernel(order, c_ref, right_ref, left_ref, code_v, weight_v, *refs):
    blocks, outs = refs[:32], refs[32 : 32 + len(order)]
    held, main_sems, *rest = refs[32 + len(order) :]
    mains = copies_of(blocks, held, main_sems, 0, BLOCK)
    for copy in mains:
        copy.start()
    far_sums(order, c_ref, right_ref, left_ref, outs, held, mains, code_v, weight_v, *rest)


def own_kernel(slots, weights, c_ref, right_ref, left_ref, code_v, weight_v, *refs):
    blocks, (far_out, near_out) = refs[:32], refs[32:34]
    held, main_sems, near_acc, near_lefts, near_rights, *rest = refs[34:]
    mains = copies_of(blocks, held, main_sems, 0, BLOCK)
    for copy in mains:
        copy.start()
    far_sums((0,), c_ref, right_ref, left_ref, (far_out,), held, mains, code_v, weight_v, *rest)
    near_sums((0,), held, slots, weights, c_ref, (near_out,), near_acc, near_lefts, near_rights)


def far_sums(order, c_ref, right_ref, left_ref, outs, held, mains, code_v, weight_v, *refs):
    acc, lefts, rights, kept, double, code_s, weight_s, sems = refs
    codes = pltpu.make_async_copy(code_v, code_s, sems.at[0])
    weights = pltpu.make_async_copy(weight_v, weight_s, sems.at[1])
    codes.start()
    weights.start()
    c = c_ref[...]
    double[0:DIM, 0:DIM] = c
    double[0:DIM, DIM:ROWS] = c
    double[DIM:ROWS, 0:DIM] = c
    double[DIM:ROWS, DIM:ROWS] = -c
    codes.wait()
    weights.wait()
    for copy in mains:
        copy.wait()
    for dy, out in zip(order, outs):

        def group(h, _):
            def links(g, _):
                d = dy * OWN + h * GROUP + g
                for k in range(6):
                    acc[k] = jnp.zeros((ROWS, DIM), F32)

                def add(e, _):
                    for n in (2 * e, 2 * e + 1):
                        code, weight = code_s[d, n], weight_s[d, n]
                        start = pl.multiple_of((code & 255) * ROWS, ROWS)
                        kind = code >> 8
                        acc[kind] = acc[kind] + weight * held[pl.ds(start, ROWS), :].astype(F32)
                    return 0

                lax.fori_loop(0, (code_s[d, DIM - 1] + 1) >> 1, add, 0)
                kept[g, 0] = acc[4] + acc[5]
                kept[g, 1] = acc[4] - acc[5]
                at = pl.multiple_of(g * ROWS, ROWS)
                lefts[0:DIM, pl.ds(at, ROWS)] = crossed((acc[0] + acc[1]).astype(BF))
                lefts[DIM:ROWS, pl.ds(at, ROWS)] = crossed((acc[2] + acc[3]).astype(BF))
                rights[pl.ds(at, ROWS), 0:DIM] = (acc[0] - acc[1]).astype(BF)
                rights[pl.ds(at, ROWS), DIM:ROWS] = (acc[2] - acc[3]).astype(BF)
                return 0

            lax.fori_loop(0, GROUP, links, 0)
            c, cc, w, wh = c_ref[...], double[...], right_ref[...], left_ref[...]
            cuts = [slice(g * ROWS, (g + 1) * ROWS) for g in range(GROUP)]
            left, right = mm(cc, lefts[...]), mm(rights[...], cc)
            halves = []
            for g, at in enumerate(cuts):
                for k in range(2):
                    side, cols = left[k * DIM : (k + 1) * DIM, at], right[at, k * DIM : (k + 1) * DIM]
                    re = kept[g, k, 0:DIM] + side[:, :DIM] - cols[DIM:]
                    im = kept[g, k, DIM:ROWS] + side[:, DIM:] + cols[:DIM]
                    halves.append(jnp.concatenate([re, im], axis=1).astype(BF))
            mid = mm(jnp.concatenate(halves), w).astype(BF)
            turned = mm(wh, jnp.concatenate([stack_parts(mid[at]) for at in cuts], axis=1)).astype(BF)
            parts = [turned[:, at] for at in cuts]
            left = mm(c, jnp.concatenate([crossed(t[:, :DIM]) for t in parts], axis=1))
            right = mm(jnp.concatenate([t[:, DIM:] for t in parts]), c)
            for g, at in enumerate(cuts):
                to = pl.multiple_of((h * GROUP + g) * ROWS, ROWS)
                out[pl.ds(to, DIM), :] = (left[:, at][:, :DIM] - right[at][DIM:]).astype(out.dtype)
                out[pl.ds(to + DIM, DIM), :] = (left[:, at][:, DIM:] + right[at][:DIM]).astype(out.dtype)
            return 0

        lax.fori_loop(0, OWN // GROUP, group, 0)


def stack_parts(mid):
    return jnp.concatenate(
        [
            jnp.concatenate([mid[:DIM, :DIM], mid[DIM:, :DIM]], axis=1),
            jnp.concatenate([mid[:DIM, DIM:], mid[DIM:, DIM:]], axis=1),
        ]
    )


SM = pl.BlockSpec(memory_space=pltpu.SMEM)
VM = pl.BlockSpec(memory_space=pltpu.VMEM)
FAR = pl.BlockSpec(memory_space=pltpu.HBM)


def part_shapes(order):
    return [jax.ShapeDtypeStruct((BLOCK, DIM), BF if dy else F32) for dy in order]


def near_scratch():
    return [pltpu.VMEM((2, ROWS, DIM), F32), pltpu.VMEM((OWN, DIM, ROWS), BF), pltpu.VMEM((OWN, ROWS, DIM), BF)]


def near_parts(order, lists, coupling, blocks):
    return pl.pallas_call(
        functools.partial(near_kernel, order),
        out_shape=part_shapes(order),
        in_specs=[SM] * 2 + [VM] + [FAR] * 32,
        out_specs=[VM] * len(order),
        scratch_shapes=[pltpu.VMEM((32 * BLOCK, DIM), BF), pltpu.SemaphoreType.DMA((32,))] + near_scratch(),
        compiler_params=pltpu.CompilerParams(vmem_limit_bytes=26 << 20),
        cost_estimate=pl.CostEstimate(flops=10**8, bytes_accessed=1 << 20, transcendentals=0),
    )(*lists, coupling, *blocks)


def far_scratch():
    return [
        pltpu.VMEM((6, ROWS, DIM), F32),
        pltpu.VMEM((ROWS, GROUP * ROWS), BF),
        pltpu.VMEM((GROUP * ROWS, ROWS), BF),
        pltpu.VMEM((GROUP, 2, ROWS, DIM), F32),
        pltpu.VMEM((ROWS, ROWS), BF),
        pltpu.SMEM((32, DIM), jnp.int32),
        pltpu.SMEM((32, DIM), F32),
        pltpu.SemaphoreType.DMA((2,)),
    ]


def held_scratch(rows):
    return [pltpu.VMEM((32 * rows, DIM), BF), pltpu.SemaphoreType.DMA((32,))]


LISTS = [jax.ShapeDtypeStruct((32, DIM), jnp.int32), jax.ShapeDtypeStruct((32, DIM), F32)]


def far_parts(order, arrays, blocks):
    return pl.pallas_call(
        functools.partial(far_kernel, order),
        out_shape=part_shapes(order) + LISTS,
        in_specs=[VM] * len(arrays) + [FAR] * 32,
        out_specs=[VM] * (len(order) + 2),
        scratch_shapes=held_scratch(BLOCK) + held_scratch(EXTRA) + far_scratch(),
        compiler_params=pltpu.CompilerParams(vmem_limit_bytes=30 << 20),
        cost_estimate=pl.CostEstimate(flops=10**8, bytes_accessed=1 << 20, transcendentals=0),
    )(*arrays, *blocks)


def more_parts(order, arrays, blocks):
    return pl.pallas_call(
        functools.partial(more_kernel, order),
        out_shape=part_shapes(order),
        in_specs=[VM] * len(arrays) + [FAR] * 32,
        out_specs=[VM] * len(order),
        scratch_shapes=held_scratch(BLOCK) + far_scratch(),
        compiler_params=pltpu.CompilerParams(vmem_limit_bytes=30 << 20),
        cost_estimate=pl.CostEstimate(flops=10**8, bytes_accessed=1 << 20, transcendentals=0),
    )(*arrays, *blocks)


def own_parts(scalars, arrays, blocks):
    return pl.pallas_call(
        own_kernel,
        out_shape=part_shapes((0, 0)),
        in_specs=[SM] * 2 + [VM] * len(arrays) + [FAR] * 32,
        out_specs=[VM] * 2,
        scratch_shapes=held_scratch(BLOCK) + near_scratch() + far_scratch(),
        compiler_params=pltpu.CompilerParams(vmem_limit_bytes=30 << 20),
        cost_estimate=pl.CostEstimate(flops=10**8, bytes_accessed=1 << 20, transcendentals=0),
    )(*scalars, *arrays, *blocks)


def chain_kernel(step, decay, lam_ref, own_ref, a_ref, b_ref, d_ref, right_ref, left_ref, saved_hbm, *refs):
    out_ref, grad_ref, wide, tall, saved_ref, sems = refs

    def saved_copy(u):
        return pltpu.make_async_copy(saved_hbm.at[step * 4 + u], saved_ref.at[u], sems.at[u])

    for u in range(4):
        saved_copy(u).start()
    for j in range(OWN):
        rows = pl.ds(j * ROWS, ROWS)
        mixed = decay[j] * lam_ref[rows, :].astype(F32) + own_ref[rows, :]
        mixed = mixed + a_ref[rows, :].astype(F32) + b_ref[rows, :].astype(F32) + d_ref[rows, :].astype(F32)
        mixed = mixed.astype(BF)
        wide[pl.ds(j * DIM, DIM), 0:DIM] = mixed[:DIM]
        wide[pl.ds(j * DIM, DIM), DIM:ROWS] = mixed[DIM:]

    def substep(u, _):
        right, left = right_ref[step * 4 + u], left_ref[step * 4 + u]
        mid = mm(wide[...], right).astype(BF)
        pairs_of = [stack_parts(mid[h * ROWS : (h + 1) * ROWS]) for h in range(OWN // 2)]
        turned = mm(left, jnp.concatenate(pairs_of, axis=1)).astype(BF)
        for j in range(OWN):
            re, im = turned[:DIM, j * DIM : (j + 1) * DIM], turned[DIM:, j * DIM : (j + 1) * DIM]
            wide[pl.ds(j * DIM, DIM), 0:DIM] = re
            wide[pl.ds(j * DIM, DIM), DIM:ROWS] = im
            tall[pl.ds(j * ROWS, DIM), 0:DIM] = re
            tall[pl.ds(j * ROWS, DIM), DIM:ROWS] = im
            tall[pl.ds(j * ROWS + DIM, DIM), 0:DIM] = im
            tall[pl.ds(j * ROWS + DIM, DIM), DIM:ROWS] = -re
        saved_copy(u).wait()
        terms = lax.dot_general(
            saved_ref[u], tall[...], (((0,), (0,)), ((), ())), preferred_element_type=F32
        )
        grad_ref[u, 0] = terms[:, :DIM]
        grad_ref[u, 1] = terms[:, DIM:]
        return 0

    lax.fori_loop(0, 4, substep, 0)
    for j in range(OWN):
        out_ref[pl.ds(j * ROWS, DIM), :] = wide[pl.ds(j * DIM, DIM), 0:DIM]
        out_ref[pl.ds(j * ROWS + DIM, DIM), :] = wide[pl.ds(j * DIM, DIM), DIM:ROWS]


def chain(step, decay, lam, parts, right, left, saved):
    return pl.pallas_call(
        functools.partial(chain_kernel, step),
        out_shape=[
            jax.ShapeDtypeStruct((BLOCK, DIM), BF),
            jax.ShapeDtypeStruct((4, 2, DIM, DIM), F32),
        ],
        in_specs=[SM] + [VM] * 7 + [FAR],
        out_specs=[VM] * 2,
        scratch_shapes=[pltpu.VMEM((OWN * DIM, ROWS), BF), pltpu.VMEM((BLOCK, ROWS), BF), pltpu.VMEM((4, BLOCK, DIM), BF), pltpu.SemaphoreType.DMA((4,))],
        compiler_params=pltpu.CompilerParams(vmem_limit_bytes=8 << 20),
        cost_estimate=pl.CostEstimate(flops=10**8, bytes_accessed=1 << 20, transcendentals=0),
    )(decay, lam, *parts, right, left, saved)


def fill_right(out, re, im):
    out[0:DIM, 0:DIM] = re
    out[0:DIM, DIM:ROWS] = im
    out[DIM:ROWS, 0:DIM] = -im
    out[DIM:ROWS, DIM:ROWS] = re


def sides_kernel(prop_ref, *refs):
    small = (len(refs) - 4) // 2
    for given, out in zip(refs[:small], refs[small + 4 :]):
        out[...] = given[...]
    whole_right, whole_left, right_ref, left_ref = refs[small : small + 4]
    for n in range(8):
        re, im = prop_ref[n, 0], prop_ref[n, 1]
        fill_right(right_ref.at[n], re, im)
        fill_right(left_ref.at[n], re.T, im.T)
    hi = lambda v: v.astype(BF)
    re, im = prop_ref[0, 0].astype(F32), prop_ref[0, 1].astype(F32)
    for u in range(1, 4):
        ur, ui = prop_ref[u, 0], prop_ref[u, 1]
        mul = lambda v, m: mm(hi(v), m) + mm(hi(v - hi(v).astype(F32)), m)
        re, im = mul(re, ur) - mul(im, ui), mul(re, ui) + mul(im, ur)
    fill_right(whole_right, hi(re), hi(im))
    fill_right(whole_left, hi(re.T), hi(im.T))


def sides(props, small):
    return pl.pallas_call(
        sides_kernel,
        out_shape=[jax.ShapeDtypeStruct((ROWS, ROWS), BF)] * 2 + [jax.ShapeDtypeStruct((8, ROWS, ROWS), BF)] * 2
        + [jax.ShapeDtypeStruct(v.shape, v.dtype) for v in small],
        in_specs=[VM] * (1 + len(small)),
        out_specs=[VM] * (4 + len(small)),
        compiler_params=pltpu.CompilerParams(vmem_limit_bytes=8 << 20),
    )(props, *small)


def body(adjoint, saved, propagators, coupling, higher, lower, ladder, rates, decay):
    at = tuple(lax.axis_index(a) for a in AXES)
    lam = adjoint.reshape(BLOCK, DIM)
    meta = jnp.pad(own_meta(ladder, decay), ((0, 0), (0, 5)))
    by_y = [meta] + [send(meta, along_y(s)) for s in (1, 2, 3)]
    ladders = jnp.concatenate([by_y[(4 - dy) % 4][:, :8] for dy in range(4)])
    tail = jnp.pad(jnp.stack(by_y).astype(BF), ((0, 0), (0, 16 - OWN), (0, DIM - 16))).reshape(EXTRA, DIM)
    weights = ladders * rates.reshape(1, 8)
    scale = link_scale(rates)

    def prepare(arrived):
        tied = (propagators, higher, lower, weights, ladders, scale, arrived)
        props, up, down, *rest, _ = lax.optimization_barrier(tied)
        return sides(props.reshape(8, 2, DIM, DIM), [*rest, *tables_of(up, down, at)])

    made, blocks = gather_layer(jnp.concatenate([lam, tail]), prepare)
    whole_right, whole_left, right, left, weights, ladders, scale, partner, rows, slots, table = made
    one_2, one_1, one_3 = near_parts((2, 1, 3), [slots, weights], coupling, blocks)
    got_one = [send(p, along_y(s)) for p, s in ((one_2, 2), (one_1, 1), (one_3, 3))]
    whole = [coupling, whole_right, whole_left]
    small = [partner, rows, ladders, scale, slots, table]
    two_2, *lists = far_parts((2,), whole + small, blocks)
    two_1, two_3 = more_parts((1, 3), whole + lists, blocks)
    got_two = [send(p, along_y(s)) for p, s in ((two_2, 2), (two_1, 1), (two_3, 3))]
    two_0, one_0 = own_parts([slots, weights], whole + lists, blocks)
    got_one, got_two = [one_0] + got_one, [two_0] + got_two
    saved = saved.reshape(8, BLOCK, DIM)
    lam, grad_one = chain(0, decay, lam, got_one, right, left, saved)
    lam, grad_two = chain(1, decay, lam, got_two, right, left, saved)
    grad = jnp.concatenate([grad_one, grad_two]).astype(BF)
    grad = jnp.moveaxis(grad, 2, 0)
    grad = lax.all_to_all(grad, AXES, 0, 0, tiled=True)
    grad = jnp.sum(grad.astype(F32), axis=0, keepdims=True)
    return lam.reshape(OWN, 2, DIM, DIM), grad


def solution(mesh):
    finer = Mesh(mesh.devices.reshape(4, 2, 4, 4), AXES)
    rows = P(AXES)
    return jax.shard_map(
        body,
        mesh=finer,
        in_specs=(rows, P(None, None, AXES), P(), P(), P(), P(), P(None, AXES), P(), rows),
        out_specs=(rows, rows),
        check_vma=False,
    )
```

```python
import functools

import jax
import jax.numpy as jnp
import numpy as np
from jax import lax
from jax.experimental import pallas as pl
from jax.experimental.pallas import tpu as pltpu
from jax.sharding import Mesh
from jax.sharding import PartitionSpec as P

AXES = ("y", "c", "z", "x")
BF = jnp.bfloat16
F32 = jnp.float32
OWN = 8
MODES = 4
DIM = 128
ROWS = 2 * DIM
BLOCK = OWN * ROWS
GROUP = 8
EXTRA = 64


def pairs(move):
    out = []
    for y in range(4):
        for c in range(2):
            for z in range(4):
                for x in range(4):
                    ny, nc, nz, nx = move(y, c, z, x)
                    here = ((y * 2 + c) * 4 + z) * 4 + x
                    there = ((ny * 2 + nc) * 4 + nz) * 4 + nx
                    out.append((here, there))
    return out


def first(s):
    return pairs(lambda y, c, z, x: (y, c, z, (x + s) % 4) if c == 0 else (y, c, (z + s) % 4, x))


def second(s):
    return pairs(lambda y, c, z, x: (y, c, (z + s) % 4, x) if c == 0 else (y, c, z, (x + s) % 4))


def along_y(s):
    return pairs(lambda y, c, z, x: ((y + s) % 4, c, z, x))


SIBLING = pairs(lambda y, c, z, x: (y, 1 - c, z, x))


def send(a, route):
    return lax.ppermute(a, AXES, route)


def gather_layer(block, prepare):
    near = {0: block}
    for s in (1, 3, 2):
        near[s] = send(block, first(s))
    held = {(0, 0): block}
    twins = {(0, 0): send(block, SIBLING)}
    held[0, 1], held[0, 3] = send(block, second(1)), send(block, second(3))
    made = prepare(twins[0, 0])
    near[1], made = lax.optimization_barrier((near[1], made))
    for s in (1, 3, 2):
        held[s, 0] = near[s]
        held[s, 1] = send(near[s], second(1))
        held[s, 3] = send(near[s], second(3))
    for s, t in ((0, 1), (1, 3), (3, 1), (2, 3)):
        held[s, 2] = send(held[s, t], second(t))
    for key, value in held.items():
        if key not in twins:
            twins[key] = send(value, SIBLING)
    spots = [(s, t) for s in range(4) for t in range(4)]
    return made, [held[k] for k in spots] + [twins[k] for k in spots]


def own_meta(ladder, decay):
    top = lax.reduce_precision(decay, 8, 7)
    mid = lax.reduce_precision(decay - top, 8, 7)
    parts = [ladder[0].astype(F32), ladder[1].astype(F32), jnp.stack([top, mid, decay - top - mid], axis=1)]
    return jnp.concatenate(parts, axis=1)


def place(q, at):
    y, c, z, x = at
    owner = q >> 3
    oy, oc, oz, ox = owner >> 5, (owner >> 4) & 1, (owner >> 2) & 3, owner & 3
    dx, dz = (x - ox) & 3, (z - oz) & 3
    s = jnp.where(oc == 0, dx, dz)
    t = jnp.where(oc == 0, dz, dx)
    other = (oc != c).astype(jnp.int32)
    return (y - oy) & 3, ((other * 16 + s * 4 + t) << 3) + (q & 7)


def slot_of(q, at):
    dy, slot = place(q, at)
    return jnp.where(dy == 0, slot, -1)


def own_links(higher, lower, at):
    y, c, z, x = at
    rows = []
    for dy in range(4):
        start = ((((y + dy) & 3) * 2 + c) * 16 + z * 4 + x) * OWN
        both = [lax.dynamic_slice_in_dim(t, start, OWN, 0) for t in (higher, lower)]
        rows.append(jnp.concatenate(both, axis=1))
    return jnp.concatenate(rows)


def tables_of(higher, lower, at):
    partner = own_links(higher, lower, at)
    dy, slot = place(partner, at)
    table = jnp.concatenate([slot_of(higher, at), slot_of(lower, at)], axis=1).astype(BF)
    rows = (slot >> 3) * EXTRA + dy * 16 + (slot & 7)
    return partner, rows, jnp.where(dy == 0, slot, -1), table


def link_scale(rates):
    lane = np.arange(DIM)
    kind, near, far = lane >> 4, lane - 64, lane < 64
    outer = np.where(far, (kind >> 1) * 4 + ((lane >> 2) & 3), near)
    inner = np.where(far, (kind & 1) * 4 + (lane & 3), -1)
    eight = rates.reshape(1, 8)
    take = lambda n: jnp.sum(jnp.where(n[:, None] == np.arange(8)[None, :], eight, 0.0), axis=1)
    return (take(outer) * jnp.where(far, take(inner), 1.0)).reshape(1, DIM)


def copies_of(blocks, held, sems, start, rows):
    return [
        pltpu.make_async_copy(b.at[pl.ds(start, rows), :], held.at[pl.ds(k * rows, rows), :], sems.at[k])
        for k, b in enumerate(blocks)
    ]


def mm(a, b):
    return jnp.dot(a, b, preferred_element_type=F32)


def crossed(plus):
    return jnp.concatenate([plus[DIM:], -plus[:DIM]], axis=1)


def near_sums(order, held, slots, weights, c_ref, outs, acc, lefts, rights):
    for dy, out in zip(order, outs):

        def links(i, _):
            d = dy * OWN + i
            acc[...] = jnp.zeros((2, ROWS, DIM), F32)
            for k in range(2 * MODES):
                slot = slots[d, k]

                @pl.when(slot >= 0)
                def _():
                    start = pl.multiple_of(slot * ROWS, ROWS)
                    acc[k // 4] = acc[k // 4] + weights[d, k] * held[pl.ds(start, ROWS), :].astype(F32)

            lefts[i] = crossed((acc[0] + acc[1]).astype(BF))
            rights[i] = (acc[0] - acc[1]).astype(BF)
            return 0

        lax.fori_loop(0, OWN, links, 0)
        c = c_ref[...]
        for i in range(OWN):
            left, right = mm(c, lefts[i]), mm(rights[i], c)
            out[pl.ds(i * ROWS, DIM), :] = (left[:, :DIM] - right[DIM:]).astype(out.dtype)
            out[pl.ds(i * ROWS + DIM, DIM), :] = (left[:, DIM:] + right[:DIM]).astype(out.dtype)


def near_kernel(order, slots, weights, c_ref, *refs):
    blocks, outs = refs[:32], refs[32 : 32 + len(order)]
    held, sems, acc, lefts, rights = refs[32 + len(order) :]
    copies = copies_of(blocks, held, sems, 0, BLOCK)
    for copy in copies:
        copy.start()
    for copy in copies:
        copy.wait()
    near_sums(order, held, slots, weights, c_ref, outs, acc, lefts, rights)


def make_lists(partner_ref, row_ref, ladder_ref, scale_ref, slot_ref, links, table, code_v, weight_v):
    lane = lax.broadcasted_iota(jnp.int32, (32, DIM), 1)
    row = lax.broadcasted_iota(jnp.int32, (DIM, DIM), 0)
    col = lax.broadcasted_iota(jnp.int32, (DIM, DIM), 1)
    wide = lax.broadcasted_iota(jnp.int32, (32, 32 * EXTRA), 1)
    index = lax.broadcasted_iota(jnp.int32, (32, links.shape[0]), 1)
    total = jnp.zeros((32, DIM), F32)
    slot = jnp.zeros((32, DIM), F32)
    for k in range(2 * MODES):
        hot = jnp.where(row_ref[:, k : k + 1] == wide, 1.0, 0.0).astype(BF)
        wanted = mm(hot, table[...])
        mine = ladder_ref[:, k : k + 1]
        target = ((k // 4) * 2 + (row >> 2)) * 16 + (k % 4) * 4 + (row & 3)
        shift = jnp.where((row < 2 * MODES) & (col == target), 1.0, 0.0).astype(BF)
        total = total + mm((wanted * mine).astype(BF), shift)
        found = jnp.where(partner_ref[:, k : k + 1] == index, 1.0, 0.0).astype(BF)
        slot = slot + mm(mm(found, links[...]).astype(BF), shift[: 2 * MODES])
        slot = jnp.where(lane == 64 + k, slot_ref[:, k : k + 1].astype(F32), slot)
        decay = wanted[:, 8:9] + wanted[:, 9:10] + wanted[:, 10:11]
        total = jnp.where(lane == 64 + k, decay * mine, total)
    keep = (lane < 72) & (slot >= 0) & (total != 0)
    kept = jnp.where(keep, 1.0, 0.0)
    spot = mm(kept.astype(BF), jnp.where(row < col, 1.0, 0.0).astype(BF)).astype(jnp.int32)
    spot = jnp.where(keep, spot, -1)
    kind = jnp.where(lane < 64, lane >> 4, 4 + ((lane - 64) >> 2)).astype(F32)
    code, weight = slot + 256.0 * kind, total * scale_ref[...]
    counts = jnp.sum(kept, axis=1, keepdims=True)

    def place_some(step, lists):
        codes, weights = lists
        for e in range(8):
            n = step * 8 + e
            here = spot == n
            one = jnp.sum(jnp.where(here, code, 0.0), axis=1, keepdims=True)
            two = jnp.sum(jnp.where(here, weight, 0.0), axis=1, keepdims=True)
            codes, weights = jnp.where(lane == n, one, codes), jnp.where(lane == n, two, weights)
        return codes, weights

    empty = (jnp.zeros((32, DIM), F32), jnp.zeros((32, DIM), F32))
    codes, weights = lax.fori_loop(0, (jnp.max(counts).astype(jnp.int32) + 7) >> 3, place_some, empty)
    codes = jnp.where(lane == DIM - 1, counts, codes)
    code_v[...] = codes.astype(jnp.int32)
    weight_v[...] = weights


def far_kernel(order, c_ref, right_ref, left_ref, *refs):
    small, blocks, refs = refs[:6], refs[6:38], refs[38:]
    outs, code_v, weight_v = refs[: len(order)], refs[len(order)], refs[len(order) + 1]
    held, main_sems, extra, extra_sems, *rest = refs[len(order) + 2 :]
    tails = copies_of(blocks, extra, extra_sems, BLOCK, EXTRA)
    mains = copies_of(blocks, held, main_sems, 0, BLOCK)
    for copy in tails + mains:
        copy.start()
    for copy in tails:
        copy.wait()
    make_lists(*small, extra, code_v, weight_v)
    far_sums(order, c_ref, right_ref, left_ref, outs, held, mains, code_v, weight_v, *rest)


def more_kernel(order, c_ref, right_ref, left_ref, code_v, weight_v, *refs):
    blocks, outs = refs[:32], refs[32 : 32 + len(order)]
    held, main_sems, *rest = refs[32 + len(order) :]
    mains = copies_of(blocks, held, main_sems, 0, BLOCK)
    for copy in mains:
        copy.start()
    far_sums(order, c_ref, right_ref, left_ref, outs, held, mains, code_v, weight_v, *rest)


def own_kernel(slots, weights, c_ref, right_ref, left_ref, code_v, weight_v, *refs):
    blocks, (far_out, near_out) = refs[:32], refs[32:34]
    held, main_sems, near_acc, near_lefts, near_rights, *rest = refs[34:]
    mains = copies_of(blocks, held, main_sems, 0, BLOCK)
    for copy in mains:
        copy.start()
    far_sums((0,), c_ref, right_ref, left_ref, (far_out,), held, mains, code_v, weight_v, *rest)
    near_sums((0,), held, slots, weights, c_ref, (near_out,), near_acc, near_lefts, near_rights)


def far_sums(order, c_ref, right_ref, left_ref, outs, held, mains, code_v, weight_v, *refs):
    acc, lefts, rights, kept, double, code_s, weight_s, sems = refs
    codes = pltpu.make_async_copy(code_v, code_s, sems.at[0])
    weights = pltpu.make_async_copy(weight_v, weight_s, sems.at[1])
    codes.start()
    weights.start()
    c = c_ref[...]
    double[0:DIM, 0:DIM] = c
    double[0:DIM, DIM:ROWS] = c
    double[DIM:ROWS, 0:DIM] = c
    double[DIM:ROWS, DIM:ROWS] = -c
    codes.wait()
    weights.wait()
    for copy in mains:
        copy.wait()
    for dy, out in zip(order, outs):

        def group(h, _):
            def links(g, _):
                d = dy * OWN + h * GROUP + g
                for k in range(6):
                    acc[k] = jnp.zeros((ROWS, DIM), F32)

                def add(e, _):
                    for n in (4 * e, 4 * e + 1, 4 * e + 2, 4 * e + 3):
                        code, weight = code_s[d, n], weight_s[d, n]
                        start = pl.multiple_of((code & 255) * ROWS, ROWS)
                        kind = code >> 8
                        acc[kind] = acc[kind] + weight * held[pl.ds(start, ROWS), :].astype(F32)
                    return 0

                lax.fori_loop(0, (code_s[d, DIM - 1] + 3) >> 2, add, 0)
                kept[g, 0] = acc[4] + acc[5]
                kept[g, 1] = acc[4] - acc[5]
                at = pl.multiple_of(g * ROWS, ROWS)
                lefts[0:DIM, pl.ds(at, ROWS)] = crossed((acc[0] + acc[1]).astype(BF))
                lefts[DIM:ROWS, pl.ds(at, ROWS)] = crossed((acc[2] + acc[3]).astype(BF))
                rights[pl.ds(at, ROWS), 0:DIM] = (acc[0] - acc[1]).astype(BF)
                rights[pl.ds(at, ROWS), DIM:ROWS] = (acc[2] - acc[3]).astype(BF)
                return 0

            lax.fori_loop(0, GROUP, links, 0)
            c, cc, w, wh = c_ref[...], double[...], right_ref[...], left_ref[...]
            cuts = [slice(g * ROWS, (g + 1) * ROWS) for g in range(GROUP)]
            left, right = mm(cc, lefts[...]), mm(rights[...], cc)
            halves = []
            for g, at in enumerate(cuts):
                for k in range(2):
                    side, cols = left[k * DIM : (k + 1) * DIM, at], right[at, k * DIM : (k + 1) * DIM]
                    re = kept[g, k, 0:DIM] + side[:, :DIM] - cols[DIM:]
                    im = kept[g, k, DIM:ROWS] + side[:, DIM:] + cols[:DIM]
                    halves.append(jnp.concatenate([re, im], axis=1).astype(BF))
            mid = mm(jnp.concatenate(halves), w).astype(BF)
            turned = mm(wh, jnp.concatenate([stack_parts(mid[at]) for at in cuts], axis=1)).astype(BF)
            parts = [turned[:, at] for at in cuts]
            left = mm(c, jnp.concatenate([crossed(t[:, :DIM]) for t in parts], axis=1))
            right = mm(jnp.concatenate([t[:, DIM:] for t in parts]), c)
            for g, at in enumerate(cuts):
                to = pl.multiple_of((h * GROUP + g) * ROWS, ROWS)
                out[pl.ds(to, DIM), :] = (left[:, at][:, :DIM] - right[at][DIM:]).astype(out.dtype)
                out[pl.ds(to + DIM, DIM), :] = (left[:, at][:, DIM:] + right[at][:DIM]).astype(out.dtype)
            return 0

        lax.fori_loop(0, OWN // GROUP, group, 0)


def stack_parts(mid):
    return jnp.concatenate(
        [
            jnp.concatenate([mid[:DIM, :DIM], mid[DIM:, :DIM]], axis=1),
            jnp.concatenate([mid[:DIM, DIM:], mid[DIM:, DIM:]], axis=1),
        ]
    )


SM = pl.BlockSpec(memory_space=pltpu.SMEM)
VM = pl.BlockSpec(memory_space=pltpu.VMEM)
FAR = pl.BlockSpec(memory_space=pltpu.HBM)


def part_shapes(order):
    return [jax.ShapeDtypeStruct((BLOCK, DIM), BF if dy else F32) for dy in order]


def near_scratch():
    return [pltpu.VMEM((2, ROWS, DIM), F32), pltpu.VMEM((OWN, DIM, ROWS), BF), pltpu.VMEM((OWN, ROWS, DIM), BF)]


def near_parts(order, lists, coupling, blocks):
    return pl.pallas_call(
        functools.partial(near_kernel, order),
        out_shape=part_shapes(order),
        in_specs=[SM] * 2 + [VM] + [FAR] * 32,
        out_specs=[VM] * len(order),
        scratch_shapes=[pltpu.VMEM((32 * BLOCK, DIM), BF), pltpu.SemaphoreType.DMA((32,))] + near_scratch(),
        compiler_params=pltpu.CompilerParams(vmem_limit_bytes=26 << 20),
        cost_estimate=pl.CostEstimate(flops=10**8, bytes_accessed=1 << 20, transcendentals=0),
    )(*lists, coupling, *blocks)


def far_scratch():
    return [
        pltpu.VMEM((6, ROWS, DIM), F32),
        pltpu.VMEM((ROWS, GROUP * ROWS), BF),
        pltpu.VMEM((GROUP * ROWS, ROWS), BF),
        pltpu.VMEM((GROUP, 2, ROWS, DIM), F32),
        pltpu.VMEM((ROWS, ROWS), BF),
        pltpu.SMEM((32, DIM), jnp.int32),
        pltpu.SMEM((32, DIM), F32),
        pltpu.SemaphoreType.DMA((2,)),
    ]


def held_scratch(rows):
    return [pltpu.VMEM((32 * rows, DIM), BF), pltpu.SemaphoreType.DMA((32,))]


LISTS = [jax.ShapeDtypeStruct((32, DIM), jnp.int32), jax.ShapeDtypeStruct((32, DIM), F32)]


def far_parts(order, arrays, blocks):
    return pl.pallas_call(
        functools.partial(far_kernel, order),
        out_shape=part_shapes(order) + LISTS,
        in_specs=[VM] * len(arrays) + [FAR] * 32,
        out_specs=[VM] * (len(order) + 2),
        scratch_shapes=held_scratch(BLOCK) + held_scratch(EXTRA) + far_scratch(),
        compiler_params=pltpu.CompilerParams(vmem_limit_bytes=30 << 20),
        cost_estimate=pl.CostEstimate(flops=10**8, bytes_accessed=1 << 20, transcendentals=0),
    )(*arrays, *blocks)


def more_parts(order, arrays, blocks):
    return pl.pallas_call(
        functools.partial(more_kernel, order),
        out_shape=part_shapes(order),
        in_specs=[VM] * len(arrays) + [FAR] * 32,
        out_specs=[VM] * len(order),
        scratch_shapes=held_scratch(BLOCK) + far_scratch(),
        compiler_params=pltpu.CompilerParams(vmem_limit_bytes=30 << 20),
        cost_estimate=pl.CostEstimate(flops=10**8, bytes_accessed=1 << 20, transcendentals=0),
    )(*arrays, *blocks)


def own_parts(scalars, arrays, blocks):
    return pl.pallas_call(
        own_kernel,
        out_shape=part_shapes((0, 0)),
        in_specs=[SM] * 2 + [VM] * len(arrays) + [FAR] * 32,
        out_specs=[VM] * 2,
        scratch_shapes=held_scratch(BLOCK) + near_scratch() + far_scratch(),
        compiler_params=pltpu.CompilerParams(vmem_limit_bytes=30 << 20),
        cost_estimate=pl.CostEstimate(flops=10**8, bytes_accessed=1 << 20, transcendentals=0),
    )(*scalars, *arrays, *blocks)


def chain_kernel(step, decay, lam_ref, own_ref, a_ref, b_ref, d_ref, right_ref, left_ref, saved_hbm, *refs):
    out_ref, grad_ref, wide, tall, saved_ref, sems = refs

    def saved_copy(u):
        return pltpu.make_async_copy(saved_hbm.at[step * 4 + u], saved_ref.at[u], sems.at[u])

    for u in range(4):
        saved_copy(u).start()
    for j in range(OWN):
        rows = pl.ds(j * ROWS, ROWS)
        mixed = decay[j] * lam_ref[rows, :].astype(F32) + own_ref[rows, :]
        mixed = mixed + a_ref[rows, :].astype(F32) + b_ref[rows, :].astype(F32) + d_ref[rows, :].astype(F32)
        mixed = mixed.astype(BF)
        wide[pl.ds(j * DIM, DIM), 0:DIM] = mixed[:DIM]
        wide[pl.ds(j * DIM, DIM), DIM:ROWS] = mixed[DIM:]

    def substep(u, _):
        right, left = right_ref[step * 4 + u], left_ref[step * 4 + u]
        mid = mm(wide[...], right).astype(BF)
        pairs_of = [stack_parts(mid[h * ROWS : (h + 1) * ROWS]) for h in range(OWN // 2)]
        turned = mm(left, jnp.concatenate(pairs_of, axis=1)).astype(BF)
        for j in range(OWN):
            re, im = turned[:DIM, j * DIM : (j + 1) * DIM], turned[DIM:, j * DIM : (j + 1) * DIM]
            wide[pl.ds(j * DIM, DIM), 0:DIM] = re
            wide[pl.ds(j * DIM, DIM), DIM:ROWS] = im
            tall[pl.ds(j * ROWS, DIM), 0:DIM] = re
            tall[pl.ds(j * ROWS, DIM), DIM:ROWS] = im
            tall[pl.ds(j * ROWS + DIM, DIM), 0:DIM] = im
            tall[pl.ds(j * ROWS + DIM, DIM), DIM:ROWS] = -re
        saved_copy(u).wait()
        terms = lax.dot_general(
            saved_ref[u], tall[...], (((0,), (0,)), ((), ())), preferred_element_type=F32
        )
        grad_ref[u, 0] = terms[:, :DIM]
        grad_ref[u, 1] = terms[:, DIM:]
        return 0

    lax.fori_loop(0, 4, substep, 0)
    for j in range(OWN):
        out_ref[pl.ds(j * ROWS, DIM), :] = wide[pl.ds(j * DIM, DIM), 0:DIM]
        out_ref[pl.ds(j * ROWS + DIM, DIM), :] = wide[pl.ds(j * DIM, DIM), DIM:ROWS]


def chain(step, decay, lam, parts, right, left, saved):
    return pl.pallas_call(
        functools.partial(chain_kernel, step),
        out_shape=[
            jax.ShapeDtypeStruct((BLOCK, DIM), BF),
            jax.ShapeDtypeStruct((4, 2, DIM, DIM), F32),
        ],
        in_specs=[SM] + [VM] * 7 + [FAR],
        out_specs=[VM] * 2,
        scratch_shapes=[pltpu.VMEM((OWN * DIM, ROWS), BF), pltpu.VMEM((BLOCK, ROWS), BF), pltpu.VMEM((4, BLOCK, DIM), BF), pltpu.SemaphoreType.DMA((4,))],
        compiler_params=pltpu.CompilerParams(vmem_limit_bytes=8 << 20),
        cost_estimate=pl.CostEstimate(flops=10**8, bytes_accessed=1 << 20, transcendentals=0),
    )(decay, lam, *parts, right, left, saved)


def fill_right(out, re, im):
    out[0:DIM, 0:DIM] = re
    out[0:DIM, DIM:ROWS] = im
    out[DIM:ROWS, 0:DIM] = -im
    out[DIM:ROWS, DIM:ROWS] = re


def sides_kernel(prop_ref, *refs):
    small = (len(refs) - 4) // 2
    for given, out in zip(refs[:small], refs[small + 4 :]):
        out[...] = given[...]
    whole_right, whole_left, right_ref, left_ref = refs[small : small + 4]
    for n in range(8):
        re, im = prop_ref[n, 0], prop_ref[n, 1]
        fill_right(right_ref.at[n], re, im)
        fill_right(left_ref.at[n], re.T, im.T)
    hi = lambda v: v.astype(BF)
    re, im = prop_ref[0, 0].astype(F32), prop_ref[0, 1].astype(F32)
    for u in range(1, 4):
        ur, ui = prop_ref[u, 0], prop_ref[u, 1]
        mul = lambda v, m: mm(hi(v), m) + mm(hi(v - hi(v).astype(F32)), m)
        re, im = mul(re, ur) - mul(im, ui), mul(re, ui) + mul(im, ur)
    fill_right(whole_right, hi(re), hi(im))
    fill_right(whole_left, hi(re.T), hi(im.T))


def sides(props, small):
    return pl.pallas_call(
        sides_kernel,
        out_shape=[jax.ShapeDtypeStruct((ROWS, ROWS), BF)] * 2 + [jax.ShapeDtypeStruct((8, ROWS, ROWS), BF)] * 2
        + [jax.ShapeDtypeStruct(v.shape, v.dtype) for v in small],
        in_specs=[VM] * (1 + len(small)),
        out_specs=[VM] * (4 + len(small)),
        compiler_params=pltpu.CompilerParams(vmem_limit_bytes=8 << 20),
    )(props, *small)


def body(adjoint, saved, propagators, coupling, higher, lower, ladder, rates, decay):
    at = tuple(lax.axis_index(a) for a in AXES)
    lam = adjoint.reshape(BLOCK, DIM)
    meta = jnp.pad(own_meta(ladder, decay), ((0, 0), (0, 5)))
    by_y = [meta] + [send(meta, along_y(s)) for s in (1, 2, 3)]
    ladders = jnp.concatenate([by_y[(4 - dy) % 4][:, :8] for dy in range(4)])
    tail = jnp.pad(jnp.stack(by_y).astype(BF), ((0, 0), (0, 16 - OWN), (0, DIM - 16))).reshape(EXTRA, DIM)
    weights = ladders * rates.reshape(1, 8)
    scale = link_scale(rates)

    def prepare(arrived):
        tied = (propagators, higher, lower, weights, ladders, scale, arrived)
        props, up, down, *rest, _ = lax.optimization_barrier(tied)
        return sides(props.reshape(8, 2, DIM, DIM), [*rest, *tables_of(up, down, at)])

    made, blocks = gather_layer(jnp.concatenate([lam, tail]), prepare)
    whole_right, whole_left, right, left, weights, ladders, scale, partner, rows, slots, table = made
    one_2, one_1, one_3 = near_parts((2, 1, 3), [slots, weights], coupling, blocks)
    got_one = [send(p, along_y(s)) for p, s in ((one_2, 2), (one_1, 1), (one_3, 3))]
    whole = [coupling, whole_right, whole_left]
    small = [partner, rows, ladders, scale, slots, table]
    two_2, *lists = far_parts((2,), whole + small, blocks)
    two_1, two_3 = more_parts((1, 3), whole + lists, blocks)
    got_two = [send(p, along_y(s)) for p, s in ((two_2, 2), (two_1, 1), (two_3, 3))]
    two_0, one_0 = own_parts([slots, weights], whole + lists, blocks)
    got_one, got_two = [one_0] + got_one, [two_0] + got_two
    saved = saved.reshape(8, BLOCK, DIM)
    lam, grad_one = chain(0, decay, lam, got_one, right, left, saved)
    lam, grad_two = chain(1, decay, lam, got_two, right, left, saved)
    grad = jnp.concatenate([grad_one, grad_two]).astype(BF)
    grad = jnp.moveaxis(grad, 2, 0)
    grad = lax.all_to_all(grad, AXES, 0, 0, tiled=True)
    grad = jnp.sum(grad.astype(F32), axis=0, keepdims=True)
    return lam.reshape(OWN, 2, DIM, DIM), grad


def solution(mesh):
    finer = Mesh(mesh.devices.reshape(4, 2, 4, 4), AXES)
    rows = P(AXES)
    return jax.shard_map(
        body,
        mesh=finer,
        in_specs=(rows, P(None, None, AXES), P(), P(), P(), P(), P(None, AXES), P(), rows),
        out_specs=(rows, rows),
        check_vma=False,
    )
```
